32 devices in a mesh: row: 4 (over z), col: 8 (over y, x, core).
Axes of the slice: x: 2, y: 2, z: 4, core: 2. Of those that a mesh axis runs over, the one named last changes fastest.
Arguments:
- tokens: bfloat16 [8192, 2048], P('row', 'col'), may hold values from -6 to 6
- cotangent: bfloat16 [8192, 2048], P('row', 'col'), may hold values from -6 to 6
- segments: int32 [8192], P('row'), may hold values from 0 to 24, never falling along the last dimension, each value on 1 to 800 neighbouring positions
- query_weight: bfloat16 [2048, 2048], P('row', 'col'), may hold values from -0.125 to 0.125
- query_bias: float32 [2048], P('col'), may hold values from -3 to 3
- key_weight: bfloat16 [2048, 2048], P('row', 'col'), may hold values from -0.125 to 0.125
- value_weight: bfloat16 [2048, 2048], P('row', 'col'), may hold values from -0.125 to 0.125
- value_bias: float32 [2048], P('col'), may hold values from -3 to 3
- output_weight: bfloat16 [2048, 2048], P('col', 'row'), may hold values from -0.5 to 0.5
- output_bias: float32 [2048], P('col'), may hold values from -3 to 3
- first_gain: float32 [2048], P('col'), may hold values from 0.5 to 1.5
- first_shift: float32 [2048], P('col'), may hold values from -1.75 to 1.75
- up_weight: bfloat16 [2048, 8192], P('row', 'col'), may hold values from -0.125 to 0.125
- up_bias: float32 [8192], P('col'), may hold values from -3 to 3
- down_weight: bfloat16 [8192, 2048], P('col', 'row'), may hold values from -0.0625 to 0.0625
- down_bias: float32 [2048], P('col'), may hold values from -3 to 3
- second_gain: float32 [2048], P('col'), may hold values from 0.5 to 1.5
- second_shift: float32 [2048], P('col'), may hold values from -1.75 to 1.75
Outputs:
- output: bfloat16 [8192, 2048], P('row', 'col')
- grad_tokens: float32 [8192, 2048], P('row', 'col')
- query_weight_grad: float32 [2048, 2048], P('row', 'col')
- query_bias_grad: float32 [2048], P('col')
- key_weight_grad: float32 [2048, 2048], P('row', 'col')
- value_weight_grad: float32 [2048, 2048], P('row', 'col')
- value_bias_grad: float32 [2048], P('col')
- output_weight_grad: float32 [2048, 2048], P('col', 'row')
- output_bias_grad: float32 [2048], P('col')
- first_gain_grad: float32 [2048], P('col')
- first_shift_grad: float32 [2048], P('col')
- up_weight_grad: float32 [2048, 8192], P('row', 'col')
- up_bias_grad: float32 [8192], P('col')
- down_weight_grad: float32 [8192, 2048], P('col', 'row')
- down_bias_grad: float32 [2048], P('col')
- second_gain_grad: float32 [2048], P('col')
- second_shift_grad: float32 [2048], P('col')
The draws below stay inside these ranges and needn't reach their ends.
Inputs may be any that keep to these rules, and one draw needn't show every extreme that they name: `segments`: document numbers never fall along the tokens; a document holds at most 800 tokens.
All inputs are finite; a program needn't handle non-finite values.
Results may differ from the reference program's by a relative error of at most 0.034.
Values may be sent and summed in bfloat16 or wider, within the bound.
No kernel may reach another device: no remote copies, remote signals or barrier semaphores. Data moves between devices by JAX's collectives and lax.ppermute only.
A program may use at most 256 MiB of HBM per device.

```python
import math
import jax
import jax.numpy as jnp
import numpy as np
from jax import lax

D = 2048
HEADS = 16
F = 8192
HEAD_DIM = 128
LAYERS = 2
SEQ_LEN = 1024
TOKENS = 8192
DOCS = 25
MOST_DOC = 800
N_COL = 8


def block_scale(own_key, extent, split, least, top_value):
    def one(axis_at, shards_of):
        steps = jax.random.uniform(jax.random.fold_in(jax.random.fold_in(own_key, 6), axis_at), (shards_of,), jnp.float32, least / len(split), top_value / len(split))
        return jnp.repeat(jnp.exp(steps), extent[axis_at] // shards_of).reshape((-1,) + (1,) * (len(extent) - axis_at - 1))

    factor_of = one(*split[0])
    for cut in split[1:]:
        factor_of = factor_of * one(*cut)
    return factor_of


def split_up(count, total, most, slope):
    loads = [(1 << 20) // math.isqrt(standing ** slope) + 1 for standing in range(2, count + 1)]
    spare, counts = total - most - (count - 1), [1] * (count - 1)
    while spare > 0:
        movable = [i for i in range(count - 1) if counts[i] < most]
        mass, left = sum([loads[i] for i in movable]), spare
        for i in movable:
            more = min(most - counts[i], max(1, left * loads[i] // mass), spare)
            counts[i] = counts[i] + more
            spare = spare - more
    return np.array([most] + counts)


def uneven_parts(stream_key, amount, total, bound, slope):
    if amount == 2:
        one = jax.random.randint(stream_key, (), max(1, total - bound), min(bound, total - 1) + 1)
        return jnp.stack([one, total - one])
    sizes = jnp.asarray(split_up(amount, total, bound, slope), jnp.int32)
    twos = (amount - 1) // 2
    donor, receiver = sizes[1:1 + 2 * twos:2], sizes[2:2 + 2 * twos:2]
    margin = jnp.minimum(donor - 1, bound - receiver)
    moved = jax.random.randint(jax.random.fold_in(stream_key, 1), (twos,), 0, 1 << 20) % (margin + 1)
    sizes = sizes.at[1:1 + 2 * twos:2].set(donor - moved).at[2:2 + 2 * twos:2].set(receiver + moved)
    return sizes[jax.random.permutation(jax.random.fold_in(stream_key, 2), amount)]


def gaussian(stream_key, shape, scale, limit, split=(), dtype=jnp.bfloat16):
    entries = jax.random.normal(stream_key, shape, jnp.float32) * scale
    if len(split) > 0:
        entries = block_scale(stream_key, shape, split, -0.22, 0.18) * entries
    return jnp.clip(entries, min=-limit, max=limit).astype(dtype)


def setup_inputs(seed: int = 0) -> dict:
    seeds = jax.random.split(jax.random.key(seed), 19)
    tokens = gaussian(seeds[0], (TOKENS, D), 1.0, 6.0, ((0, 4), (1, 8)))
    cotangent = gaussian(seeds[1], (TOKENS, D), 1.0, 6.0, ((0, 4), (1, 8)))
    segments = jnp.searchsorted(jnp.cumsum(uneven_parts(seeds[2], DOCS, TOKENS, MOST_DOC, 0)), jnp.arange(TOKENS), side="right").astype(jnp.int32)
    query_weight = gaussian(seeds[3], (D, D), D ** -0.5, 0.125, ((0, 4), (1, 8)))
    query_bias = gaussian(seeds[4], (D,), 0.5, 3.0, ((0, 8),), jnp.float32)
    key_weight = gaussian(seeds[5], (D, D), D ** -0.5, 0.125, ((0, 4), (1, 8)))
    value_weight = gaussian(seeds[6], (D, D), D ** -0.5, 0.125, ((0, 4), (1, 8)))
    value_bias = gaussian(seeds[7], (D,), 0.5, 3.0, ((0, 8),), jnp.float32)
    output_weight = gaussian(seeds[8], (D, D), (D // 16) ** -0.5, 0.5, ((0, 8), (1, 4)))
    output_bias = gaussian(seeds[9], (D,), 0.5, 3.0, ((0, 8),), jnp.float32)
    first_gain = jnp.clip(1.0 + 0.1 * jax.random.normal(seeds[10], (D,), jnp.float32), 0.5, 1.5)
    first_shift = gaussian(seeds[11], (D,), 0.3, 1.75, ((0, 8),), jnp.float32)
    up_weight = gaussian(seeds[12], (D, F), D ** -0.5, 0.125, ((0, 4), (1, 8)))
    up_bias = gaussian(seeds[13], (F,), 0.5, 3.0, ((0, 8),), jnp.float32)
    down_weight = gaussian(seeds[14], (F, D), F ** -0.5, 0.0625, ((0, 8), (1, 4)))
    down_bias = gaussian(seeds[15], (D,), 0.5, 3.0, ((0, 8),), jnp.float32)
    second_gain = jnp.clip(1.0 + 0.1 * jax.random.normal(seeds[16], (D,), jnp.float32), 0.5, 1.5)
    second_shift = gaussian(seeds[17], (D,), 0.3, 1.75, ((0, 8),), jnp.float32)
    return dict(tokens=tokens, cotangent=cotangent, segments=segments, query_weight=query_weight, query_bias=query_bias, key_weight=key_weight, value_weight=value_weight, value_bias=value_bias, output_weight=output_weight, output_bias=output_bias, first_gain=first_gain, first_shift=first_shift, up_weight=up_weight, up_bias=up_bias, down_weight=down_weight, down_bias=down_bias, second_gain=second_gain, second_shift=second_shift)


@jax.custom_vjp
def low(v):
    return lax.optimization_barrier(v.astype(jnp.bfloat16)).astype(jnp.float32)

@jax.custom_vjp
def low_back(v):
    return v

def low_keep(v):
    return (low(v), None)

def low_pass(kept, grad):
    return (grad,)

def back_keep(v):
    return (v, None)

def back_low(kept, grad):
    return (low(grad),)
low.defvjp(low_keep, low_pass)
low_back.defvjp(back_keep, back_low)
highest = lax.Precision.HIGHEST
epsilon = 1e-06
masked_score = -1e+30

def product(left, right):
    return jnp.dot(left, right, precision=highest, preferred_element_type=jnp.float32)

def split_sum(left, right):
    rows, inner = left.shape
    width = inner // N_COL
    pieces = left.reshape(rows, N_COL, width)
    blocks = right.reshape(N_COL, width, right.shape[1])
    terms = jnp.einsum('tkc,kcd->ktd', pieces, blocks, precision=highest)
    return lax.optimization_barrier(jnp.sum(low(terms), axis=0))

def normalize(residual, gain, shift):
    center = residual - lax.optimization_barrier(jnp.mean(residual, axis=-1, keepdims=True))
    spread = lax.optimization_barrier(jnp.mean(center * center, axis=-1, keepdims=True))
    return center * lax.rsqrt(spread + epsilon) * gain + shift

def attend(pieces):
    queries, keys, values, numbers = pieces
    scores = jnp.einsum('qhd,khd->hqk', queries, keys, precision=highest) * HEAD_DIM ** (-0.5)
    scores = low_back(scores)
    allowed = numbers[:, None] == numbers[None, :]
    probs = low(jax.nn.softmax(jnp.where(allowed[None], scores, masked_score), axis=-1))
    return jnp.einsum('hqk,khd->qhd', probs, values, precision=highest)

def layer(inputs, numbers, params):
    query_weight, query_bias, key_weight, value_weight, value_bias, output_weight, output_bias, first_gain, first_shift, up_weight, up_bias, down_weight, down_bias, second_gain, second_shift = params
    rounded = low(inputs)
    queries = low(low_back(product(rounded, query_weight) + query_bias))
    keys = low(low_back(product(rounded, key_weight)))
    values = low(low_back(product(rounded, value_weight) + value_bias))
    shaped = (queries.reshape(-1, SEQ_LEN, HEADS, HEAD_DIM), keys.reshape(-1, SEQ_LEN, HEADS, HEAD_DIM), values.reshape(-1, SEQ_LEN, HEADS, HEAD_DIM), numbers.reshape(-1, SEQ_LEN))
    mixed = lax.map(jax.checkpoint(attend), shaped).reshape(-1, D)
    mixed = low(low_back(mixed))
    branch = low_back(split_sum(mixed, output_weight) + output_bias)
    first = normalize(inputs + branch, first_gain, first_shift)
    hidden = low_back(product(low(first), up_weight) + up_bias)
    active = low(jax.nn.gelu(hidden, approximate=True))
    second = low_back(split_sum(active, down_weight) + down_bias)
    return normalize(first + second, second_gain, second_shift)

def reference(tokens, cotangent, segments, query_weight, query_bias, key_weight, value_weight, value_bias, output_weight, output_bias, first_gain, first_shift, up_weight, up_bias, down_weight, down_bias, second_gain, second_shift):
    params = tuple((item.astype(jnp.float32) for item in (query_weight, query_bias, key_weight, value_weight, value_bias, output_weight, output_bias, first_gain, first_shift, up_weight, up_bias, down_weight, down_bias, second_gain, second_shift)))

    def forward(inputs, weights):
        state = inputs
        for depth in range(LAYERS):
            state = layer(state, segments, weights)
        return state
    result, pull = jax.vjp(forward, tokens.astype(jnp.float32), params)
    grads = pull(cotangent.astype(jnp.float32))
    weight_grads = grads[1]
    return (result.astype(jnp.bfloat16), grads[0], weight_grads[0], weight_grads[1], weight_grads[2], weight_grads[3], weight_grads[4], weight_grads[5], weight_grads[6], weight_grads[7], weight_grads[8], weight_grads[9], weight_grads[10], weight_grads[11], weight_grads[12], weight_grads[13], weight_grads[14])
```

```python
import functools

import jax
import jax.numpy as jnp
from jax import lax
from jax.experimental import pallas as pl
from jax.experimental.pallas import tpu as pltpu
from jax.sharding import PartitionSpec as P

HEAD_DIM = 128
LAYERS = 2
SEQ_LEN = 1024

EPSILON = 1e-06
MASKED = -1e30
SCALE = HEAD_DIM ** (-0.5)

bf16 = jnp.bfloat16
f32 = jnp.float32


def dot(left, right):
    return lax.dot_general(left, right, (((1,), (0,)), ((), ())), preferred_element_type=f32)


def dot_t(left, right):
    return lax.dot_general(left, right, (((1,), (1,)), ((), ())), preferred_element_type=f32)


def dot_g(left, right):
    return lax.dot_general(left, right, (((0,), (0,)), ((), ())), preferred_element_type=f32)


def attend_kernel(qkv_ref, docs_row_ref, docs_col_ref, mixed_ref, log_ref):
    step = 256
    span = mixed_ref.shape[1]
    key_docs = docs_col_ref[...]
    for head in range(span // HEAD_DIM):
        low = head * HEAD_DIM
        keys = qkv_ref[:, span + low : span + low + HEAD_DIM]
        values_t = qkv_ref[:, 2 * span + low : 2 * span + low + HEAD_DIM].T
        for start in range(0, SEQ_LEN, step):
            query = qkv_ref[start : start + step, low : low + HEAD_DIM]
            scores = dot_t(keys, query) * SCALE
            allowed = key_docs == docs_row_ref[:, start : start + step]
            scores = jnp.where(allowed, scores, MASKED)
            peak = jnp.max(scores, axis=0, keepdims=True)
            weight = jnp.exp(scores - peak)
            total = jnp.sum(weight, axis=0, keepdims=True)
            mixed_t = dot(values_t, weight.astype(bf16)) * (1.0 / total)
            mixed_ref[start : start + step, low : low + HEAD_DIM] = mixed_t.T.astype(bf16)
            log_ref[head, :, start : start + step] = peak + jnp.log(total)


def attend(qkv, span, docs_row, docs_col):
    groups = qkv.shape[1] // (3 * span)
    heads = span // HEAD_DIM
    return pl.pallas_call(
        attend_kernel,
        grid=(groups,),
        in_specs=[
            pl.BlockSpec((SEQ_LEN, 3 * span), lambda g: (0, g)),
            pl.BlockSpec((1, SEQ_LEN), lambda g: (0, 0)),
            pl.BlockSpec((SEQ_LEN, 1), lambda g: (0, 0)),
        ],
        out_specs=[
            pl.BlockSpec((SEQ_LEN, span), lambda g: (0, g)),
            pl.BlockSpec((heads, 1, SEQ_LEN), lambda g: (g, 0, 0)),
        ],
        out_shape=[
            jax.ShapeDtypeStruct((SEQ_LEN, span * groups), bf16),
            jax.ShapeDtypeStruct((heads * groups, 1, SEQ_LEN), f32),
        ],
        compiler_params=pltpu.CompilerParams(vmem_limit_bytes=48 * 1024 * 1024),
        cost_estimate=pl.CostEstimate(
            flops=groups * heads * 8 * SEQ_LEN * SEQ_LEN * HEAD_DIM,
            bytes_accessed=groups * SEQ_LEN * span * 8,
            transcendentals=groups * heads * SEQ_LEN * SEQ_LEN,
        ),
        name="attend",
    )(qkv, docs_row, docs_col)


def attend_back_kernel(
    qkv_ref, grad_ref, log_ref, docs_row_ref, docs_col_ref, out_ref, probs_ref, dscores_ref
):
    step = 256
    span = grad_ref.shape[1]
    key_docs = docs_col_ref[...]
    for head in range(span // HEAD_DIM):
        low = head * HEAD_DIM
        own = slice(low, low + HEAD_DIM)
        keys = qkv_ref[:, span + low : span + low + HEAD_DIM]
        values = qkv_ref[:, 2 * span + low : 2 * span + low + HEAD_DIM]
        for start in range(0, SEQ_LEN, step):
            at = slice(start, start + step)
            scores = dot_t(keys, qkv_ref[at, own]) * SCALE
            allowed = key_docs == docs_row_ref[:, at]
            probs = jnp.exp(jnp.where(allowed, scores, MASKED) - log_ref[head, :, at])
            dprobs = dot_t(values, grad_ref[at, own])
            along = jnp.sum(dprobs * probs, axis=0, keepdims=True)
            probs_ref[:, at] = probs.astype(bf16)
            dscores_ref[:, at] = (probs * (dprobs - along)).astype(bf16)
        dscores = dscores_ref[...]
        out_ref[:, own] = (dot(keys.T, dscores) * SCALE).T.astype(bf16)
        out_ref[:, span + low : span + low + HEAD_DIM] = (
            dot(dscores, qkv_ref[:, own]) * SCALE
        ).astype(bf16)
        out_ref[:, 2 * span + low : 2 * span + low + HEAD_DIM] = dot(
            probs_ref[...], grad_ref[:, own]
        ).astype(bf16)


def attend_back(qkv, grad, log_total, span, docs_row, docs_col):
    groups = qkv.shape[1] // (3 * span)
    heads = span // HEAD_DIM
    return pl.pallas_call(
        attend_back_kernel,
        grid=(groups,),
        in_specs=[
            pl.BlockSpec((SEQ_LEN, 3 * span), lambda g: (0, g)),
            pl.BlockSpec((SEQ_LEN, span), lambda g: (0, g)),
            pl.BlockSpec((heads, 1, SEQ_LEN), lambda g: (g, 0, 0)),
            pl.BlockSpec((1, SEQ_LEN), lambda g: (0, 0)),
            pl.BlockSpec((SEQ_LEN, 1), lambda g: (0, 0)),
        ],
        out_specs=pl.BlockSpec((SEQ_LEN, 3 * span), lambda g: (0, g)),
        out_shape=jax.ShapeDtypeStruct((SEQ_LEN, 3 * span * groups), bf16),
        scratch_shapes=[pltpu.VMEM((SEQ_LEN, SEQ_LEN), bf16)] * 2,
        compiler_params=pltpu.CompilerParams(vmem_limit_bytes=48 * 1024 * 1024),
        cost_estimate=pl.CostEstimate(
            flops=groups * heads * 20 * SEQ_LEN * SEQ_LEN * HEAD_DIM,
            bytes_accessed=groups * SEQ_LEN * span * 16,
            transcendentals=groups * heads * SEQ_LEN * SEQ_LEN,
        ),
        name="attend_back",
    )(qkv, grad, log_total, docs_row, docs_col)


class Place:
    def __init__(self, mesh):
        self.rows = mesh.shape["row"]
        self.cols = mesh.shape["col"]
        self.a = self.cols // 2
        self.b = self.cols // 4
        self.rest = []
        mask = 1
        while mask < self.b:
            self.rest.append(mask)
            mask *= 2
        self.row = lax.axis_index("row")
        self.col = lax.axis_index("col")
        order = [0]
        for mask in self.rest:
            order = order + [item ^ mask for item in order]
        self.order = order

    def bit(self, mask):
        return (self.col // mask) % 2

    def swap(self, value, mask):
        return lax.ppermute(value, "col", [(i, i ^ mask) for i in range(self.cols)])

    def shift(self, value):
        return lax.ppermute(value, "row", [(i, (i + 1) % self.rows) for i in range(self.rows)])


    def near(self, value):
        for mask in self.rest:
            value = jnp.concatenate([value, self.swap(value, mask)], axis=0)
        return value

    def gather(self, value, far):
        other = self.swap(value, far)
        return (self.near(value), self.near(other))

    def near_sum(self, terms):
        for mask in reversed(self.rest):
            half = terms.shape[0] // 2
            got = self.swap(terms[half:].astype(bf16), mask)
            terms = terms[:half].astype(f32) + got.astype(f32)
        return terms

    def scatter(self, own, other, far):
        sent = self.swap(self.near_sum(other).astype(bf16), far)
        return self.near_sum(own) + sent.astype(f32)


    def ordered(self, mine, got, mask, axis):
        low = self.bit(mask) == 0
        return jnp.concatenate(
            [jnp.where(low, mine, got), jnp.where(low, got, mine)], axis=axis
        )

    def to_tokens(self, value):
        own = value.shape[0] // self.cols
        for mask in self.rest + [self.b, self.a]:
            width = value.shape[-1]
            split = value.reshape(-1, 2, own, width)
            bit = self.bit(mask)
            mine = lax.dynamic_index_in_dim(split, bit, 1, keepdims=False).reshape(-1, width)
            sent = lax.dynamic_index_in_dim(split, 1 - bit, 1, keepdims=False).reshape(-1, width)
            value = self.ordered(mine, self.swap(sent, mask), mask, 1)
        return value

    def to_features(self, value):
        own, width = value.shape
        value = value[None]
        for mask in [self.a, self.b] + self.rest[::-1]:
            width = width // 2
            bit = self.bit(mask)
            mine = lax.dynamic_slice_in_dim(value, bit * width, width, 2)
            sent = lax.dynamic_slice_in_dim(value, (1 - bit) * width, width, 2)
            got = self.swap(sent, mask)
            value = self.ordered(mine[:, None], got[:, None], mask, 1)
            value = value.reshape(-1, own, width)
        return value.reshape(-1, width)

    def all_features(self, value):
        for mask in self.rest + [self.b, self.a]:
            value = self.ordered(value, self.swap(value, mask), mask, 1)
        return value


    def weight(self, block, far, axis):
        other_axis = 1 - axis
        size, span = block.shape[axis], block.shape[other_axis]
        shape = [0, 0]
        shape[axis], shape[other_axis] = self.rows * size, 2 * span
        whole = jnp.zeros(shape, block.dtype)
        for step in range(self.rows):
            at = ((self.row - step + self.rows) % self.rows) * size
            other = self.swap(block, far)
            start = [0, 0]
            start[axis] = at
            whole = lax.dynamic_update_slice(whole, block, start)
            start[other_axis] = span
            whole = lax.dynamic_update_slice(whole, other, start)
            if step < self.rows - 1:
                block = self.shift(block)
        return whole

    def weight_sum(self, own, other, far, axis):
        size = own.shape[axis] // self.rows
        total = None
        for step in range(self.rows):
            at = ((self.row - 1 - step + 2 * self.rows) % self.rows) * size
            sent = lax.dynamic_slice_in_dim(other, at, size, axis).astype(bf16)
            part = lax.dynamic_slice_in_dim(own, at, size, axis) + self.swap(sent, far).astype(f32)
            if total is not None:
                part = part + self.shift(total.astype(bf16)).astype(f32)
            total = part
        return total

    def row_sum(self, value):
        mask = 1
        while mask < self.rows:
            value = value + lax.ppermute(
                value, "row", [(i, i ^ mask) for i in range(self.rows)]
            )
            mask *= 2
        return value


def norm_forward(residual, gain, shift):
    mean = jnp.mean(residual, axis=1, keepdims=True)
    center = residual - mean
    inverse = lax.rsqrt(jnp.mean(center * center, axis=1, keepdims=True) + EPSILON)
    normed = center * inverse
    return (normed * gain + shift, normed, inverse)


def norm_backward(grad, normed, inverse, gain):
    scaled = grad * gain
    mean = jnp.mean(scaled, axis=1, keepdims=True)
    along = jnp.mean(scaled * normed, axis=1, keepdims=True)
    result = inverse * (scaled - mean - normed * along)
    return (result, jnp.sum(grad * normed, axis=0), jnp.sum(grad, axis=0))


def gelu(value):
    return jax.nn.gelu(value, approximate=True)


def gelu_slope(value):
    inner = 0.7978845608028654
    cubic = 0.044715
    square = value * value
    tangent = jnp.tanh(inner * value * (1.0 + cubic * square))
    return 0.5 * (1.0 + tangent) + 0.5 * value * (1.0 - tangent * tangent) * inner * (
        1.0 + 3.0 * cubic * square
    )


def layer_forward(place, state, docs, weights, vectors):
    w_qkv, w_out, w_up, w_down = weights
    b_qkv, b_out, gain1, shift1, b_up, b_down, gain2, shift2 = vectors
    own, other = place.gather(state.astype(bf16), place.b)
    qkv_own = (dot(own, w_qkv) + b_qkv).astype(bf16)
    qkv_other = (dot(other, w_qkv) + b_qkv).astype(bf16)
    qkv = jnp.concatenate([qkv_own, qkv_other], axis=0)
    mixed, log_total = attend(qkv, w_out.shape[0] // 2, *docs)
    half = mixed.shape[0] // 2
    terms_other = dot(mixed[half:], w_out).astype(bf16)
    terms_own = dot(mixed[:half], w_out).astype(bf16)
    branch = place.scatter(terms_own, terms_other, place.b) + b_out
    first, normed1, inverse1 = norm_forward(state + branch, gain1, shift1)
    first_own, first_other = place.gather(first.astype(bf16), place.a)
    hidden_own = dot(first_own, w_up) + b_up
    hidden_other = dot(first_other, w_up) + b_up
    active_own = gelu(hidden_own).astype(bf16)
    active_other = gelu(hidden_other).astype(bf16)
    terms_other = dot(active_other, w_down).astype(bf16)
    terms_own = dot(active_own, w_down).astype(bf16)
    second = place.scatter(terms_own, terms_other, place.a) + b_down
    result, normed2, inverse2 = norm_forward(first + second, gain2, shift2)
    saved = (
        (own, other),
        qkv,
        mixed,
        log_total,
        normed1,
        inverse1,
        (first_own, first_other),
        (hidden_own, hidden_other),
        (active_own, active_other),
        normed2,
        inverse2,
    )
    return (result, saved)


def join(pair):
    return jnp.concatenate(pair, axis=0)


def layer_backward(place, grad, docs, weights, vectors, saved):
    w_qkv, w_out, w_up, w_down = weights
    b_qkv, b_out, gain1, shift1, b_up, b_down, gain2, shift2 = vectors
    tokens, qkv, mixed, log_total, normed1, inverse1, firsts, hiddens, actives, normed2, inverse2 = saved
    dr2, gain2_grad, shift2_grad = norm_backward(grad, normed2, inverse2, gain2)
    dsecond = dr2.astype(bf16)
    seconds = place.gather(dsecond, place.a)
    dhid = tuple(
        (dot_t(second, w_down) * gelu_slope(hidden)).astype(bf16)
        for second, hidden in zip(seconds, hiddens)
    )
    terms = tuple(dot_t(part, w_up).astype(bf16) for part in dhid)
    dfirst = dr2 + place.scatter(terms[0], terms[1], place.a)
    down_grad = dot_g(join(actives), join(seconds))
    dhidden = join(dhid)
    up_grad = dot_g(join(firsts), dhidden)
    dr1, gain1_grad, shift1_grad = norm_backward(dfirst, normed1, inverse1, gain1)
    dbranch = dr1.astype(bf16)
    branches = place.gather(dbranch, place.b)
    branch = join(branches)
    dmixed = join([dot_t(part, w_out).astype(bf16) for part in branches])
    out_grad = dot_g(mixed, branch)
    dqkv = attend_back(qkv, dmixed, log_total, w_out.shape[0] // 2, *docs)
    half = dqkv.shape[0] // 2
    terms_other = dot_t(dqkv[half:], w_qkv).astype(bf16)
    terms_own = dot_t(dqkv[:half], w_qkv).astype(bf16)
    dx = dr1 + place.scatter(terms_own, terms_other, place.b)
    qkv_grad = dot_g(join(tokens), dqkv)
    token_sums = jnp.stack(
        [
            jnp.sum(dbranch, axis=0, dtype=f32),
            gain1_grad,
            shift1_grad,
            jnp.sum(dsecond, axis=0, dtype=f32),
            gain2_grad,
            shift2_grad,
        ]
    )
    sums = (
        qkv_grad,
        out_grad,
        up_grad,
        down_grad,
        token_sums,
        jnp.sum(dqkv, axis=0, dtype=f32),
        jnp.sum(dhidden, axis=0, dtype=f32),
    )
    return (dx, sums)


def local(
    mesh,
    tokens,
    cotangent,
    segments,
    query_weight,
    query_bias,
    key_weight,
    value_weight,
    value_bias,
    output_weight,
    output_bias,
    first_gain,
    first_shift,
    up_weight,
    up_bias,
    down_weight,
    down_bias,
    second_gain,
    second_shift,
):
    place = Place(mesh)
    span = query_weight.shape[1]
    hidden_span = up_weight.shape[1]
    own = tokens.shape[0] // place.cols

    state = place.to_tokens(tokens).astype(f32)
    masks = place.order + [item ^ place.b for item in place.order]
    docs = jnp.concatenate(
        [
            lax.dynamic_slice_in_dim(segments, jnp.bitwise_xor(place.col, mask) * own, own, 0)
            for mask in masks
        ]
    )
    docs = (docs[None, :], docs[:, None])

    vectors = place.all_features(
        jnp.stack([output_bias, first_gain, first_shift, down_bias, second_gain, second_shift])
    )
    pair = jnp.concatenate([query_bias, jnp.zeros_like(query_bias), value_bias])
    b_qkv = jnp.concatenate([pair, place.swap(pair, place.a)])
    b_up = jnp.concatenate([up_bias, place.swap(up_bias, place.b)])
    vectors = (b_qkv, vectors[0], vectors[1], vectors[2], b_up, vectors[3], vectors[4], vectors[5])

    w_qkv = place.weight(
        jnp.concatenate([query_weight, key_weight, value_weight], axis=1), place.a, 0
    )
    w_out = place.weight(output_weight, place.a, 1)
    w_up = place.weight(up_weight, place.b, 0)
    w_down = place.weight(down_weight, place.b, 1)
    weights = (w_qkv, w_out, w_up, w_down)

    kept = []
    for depth in range(LAYERS):
        state, saved = layer_forward(place, state, docs, weights, vectors)
        kept.append(saved)
    output = place.to_features(state.astype(bf16))

    grad = place.to_tokens(cotangent).astype(f32)
    totals = None
    for depth in reversed(range(LAYERS)):
        grad, sums = layer_backward(place, grad, docs, weights, vectors, kept[depth])
        totals = sums if totals is None else tuple(x + y for x, y in zip(totals, sums))
    grad_tokens = place.to_features(grad.astype(bf16)).astype(f32)

    qkv_grad, out_grad, up_grad, down_grad, token_sums, qkv_sums, hidden_sums = totals
    down = place.weight_sum(
        down_grad[:hidden_span], down_grad[hidden_span:], place.b, 1
    )
    up = place.weight_sum(up_grad[:, :hidden_span], up_grad[:, hidden_span:], place.b, 0)
    out = place.weight_sum(out_grad[:span], out_grad[span:], place.a, 1)
    qkv = place.weight_sum(
        qkv_grad[:, : 3 * span], qkv_grad[:, 3 * span :], place.a, 0
    )

    for mask in [place.a, place.b] + place.rest[::-1]:
        width = token_sums.shape[1] // 2
        bit = place.bit(mask)
        mine = lax.dynamic_slice_in_dim(token_sums, bit * width, width, 1)
        sent = lax.dynamic_slice_in_dim(token_sums, (1 - bit) * width, width, 1)
        token_sums = mine + place.swap(sent, mask)
    qkv_sums = qkv_sums[: 3 * span] + place.swap(qkv_sums[3 * span :], place.a)
    hidden_sums = hidden_sums[:hidden_span] + place.swap(hidden_sums[hidden_span:], place.b)
    sums = place.row_sum(
        jnp.concatenate([token_sums.reshape(-1), qkv_sums, hidden_sums])
    )
    token_sums = sums[: 6 * span].reshape(6, span)
    qkv_sums = sums[6 * span : 9 * span]
    hidden_sums = sums[9 * span :]
    return (
        output,
        grad_tokens,
        qkv[:, :span],
        qkv_sums[:span],
        qkv[:, span : 2 * span],
        qkv[:, 2 * span :],
        qkv_sums[2 * span :],
        out,
        token_sums[0],
        token_sums[1],
        token_sums[2],
        up,
        hidden_sums,
        down,
        token_sums[3],
        token_sums[4],
        token_sums[5],
    )


def solution(mesh):
    both, col, back = P("row", "col"), P("col"), P("col", "row")
    return jax.shard_map(
        functools.partial(local, mesh),
        mesh=mesh,
        in_specs=(
            both, both, P("row"), both, col, both, both, col, back, col, col, col, both, col, back,
            col, col, col,
        ),
        out_specs=(
            both, both, both, col, both, both, col, back, col, col, col, both, col, back, col, col,
            col,
        ),
        check_vma=False,
    )
```

```python
import functools

import jax
import jax.numpy as jnp
from jax import lax
from jax.experimental import pallas as pl
from jax.experimental.pallas import tpu as pltpu
from jax.sharding import PartitionSpec as P

HEAD_DIM = 128
LAYERS = 2
SEQ_LEN = 1024

EPSILON = 1e-06
MASKED = -1e30
SCALE = HEAD_DIM ** (-0.5)

bf16 = jnp.bfloat16
f32 = jnp.float32


def dot(left, right):
    return lax.dot_general(left, right, (((1,), (0,)), ((), ())), preferred_element_type=f32)


def dot_t(left, right):
    return lax.dot_general(left, right, (((1,), (1,)), ((), ())), preferred_element_type=f32)


def dot_g(left, right):
    return lax.dot_general(left, right, (((0,), (0,)), ((), ())), preferred_element_type=f32)


def after(value, *others):
    others = [item for item in others if item is not None]
    if not others:
        return value
    return lax.optimization_barrier((value, others))[0]


def attend_kernel(qkv_ref, docs_row_ref, docs_col_ref, mixed_ref, log_ref):
    step = 256
    span = mixed_ref.shape[1]
    key_docs = docs_col_ref[...]
    for head in range(span // HEAD_DIM):
        low = head * HEAD_DIM
        keys = qkv_ref[:, span + low : span + low + HEAD_DIM]
        values_t = qkv_ref[:, 2 * span + low : 2 * span + low + HEAD_DIM].T
        for start in range(0, SEQ_LEN, step):
            query = qkv_ref[start : start + step, low : low + HEAD_DIM]
            scores = dot_t(keys, query) * SCALE
            allowed = key_docs == docs_row_ref[:, start : start + step]
            scores = jnp.where(allowed, scores, MASKED)
            peak = jnp.max(scores, axis=0, keepdims=True)
            weight = jnp.exp(scores - peak)
            total = jnp.sum(weight, axis=0, keepdims=True)
            mixed_t = dot(values_t, weight.astype(bf16)) * (1.0 / total)
            mixed_ref[start : start + step, low : low + HEAD_DIM] = mixed_t.T.astype(bf16)
            log_ref[head, :, start : start + step] = peak + jnp.log(total)


def attend(qkv, span, docs_row, docs_col):
    groups = qkv.shape[1] // (3 * span)
    heads = span // HEAD_DIM
    return pl.pallas_call(
        attend_kernel,
        grid=(groups,),
        in_specs=[
            pl.BlockSpec((SEQ_LEN, 3 * span), lambda g: (0, g)),
            pl.BlockSpec((1, SEQ_LEN), lambda g: (0, 0)),
            pl.BlockSpec((SEQ_LEN, 1), lambda g: (0, 0)),
        ],
        out_specs=[
            pl.BlockSpec((SEQ_LEN, span), lambda g: (0, g)),
            pl.BlockSpec((heads, 1, SEQ_LEN), lambda g: (g, 0, 0)),
        ],
        out_shape=[
            jax.ShapeDtypeStruct((SEQ_LEN, span * groups), bf16),
            jax.ShapeDtypeStruct((heads * groups, 1, SEQ_LEN), f32),
        ],
        compiler_params=pltpu.CompilerParams(vmem_limit_bytes=48 * 1024 * 1024),
        cost_estimate=pl.CostEstimate(
            flops=groups * heads * 8 * SEQ_LEN * SEQ_LEN * HEAD_DIM,
            bytes_accessed=groups * SEQ_LEN * span * 8,
            transcendentals=groups * heads * SEQ_LEN * SEQ_LEN,
        ),
        name="attend",
    )(qkv, docs_row, docs_col)


def attend_back_kernel(
    qkv_ref, grad_ref, log_ref, docs_row_ref, docs_col_ref, out_ref, probs_ref, dscores_ref
):
    step = 256
    span = grad_ref.shape[1]
    key_docs = docs_col_ref[...]
    for head in range(span // HEAD_DIM):
        low = head * HEAD_DIM
        own = slice(low, low + HEAD_DIM)
        keys = qkv_ref[:, span + low : span + low + HEAD_DIM]
        values = qkv_ref[:, 2 * span + low : 2 * span + low + HEAD_DIM]
        for start in range(0, SEQ_LEN, step):
            at = slice(start, start + step)
            scores = dot_t(keys, qkv_ref[at, own]) * SCALE
            allowed = key_docs == docs_row_ref[:, at]
            probs = jnp.exp(jnp.where(allowed, scores, MASKED) - log_ref[head, :, at])
            dprobs = dot_t(values, grad_ref[at, own])
            along = jnp.sum(dprobs * probs, axis=0, keepdims=True)
            probs_ref[:, at] = probs.astype(bf16)
            dscores_ref[:, at] = (probs * (dprobs - along)).astype(bf16)
        dscores = dscores_ref[...]
        out_ref[:, own] = (dot(keys.T, dscores) * SCALE).T.astype(bf16)
        out_ref[:, span + low : span + low + HEAD_DIM] = (
            dot(dscores, qkv_ref[:, own]) * SCALE
        ).astype(bf16)
        out_ref[:, 2 * span + low : 2 * span + low + HEAD_DIM] = dot(
            probs_ref[...], grad_ref[:, own]
        ).astype(bf16)


def attend_back(qkv, grad, log_total, span, docs_row, docs_col):
    groups = qkv.shape[1] // (3 * span)
    heads = span // HEAD_DIM
    return pl.pallas_call(
        attend_back_kernel,
        grid=(groups,),
        in_specs=[
            pl.BlockSpec((SEQ_LEN, 3 * span), lambda g: (0, g)),
            pl.BlockSpec((SEQ_LEN, span), lambda g: (0, g)),
            pl.BlockSpec((heads, 1, SEQ_LEN), lambda g: (g, 0, 0)),
            pl.BlockSpec((1, SEQ_LEN), lambda g: (0, 0)),
            pl.BlockSpec((SEQ_LEN, 1), lambda g: (0, 0)),
        ],
        out_specs=pl.BlockSpec((SEQ_LEN, 3 * span), lambda g: (0, g)),
        out_shape=jax.ShapeDtypeStruct((SEQ_LEN, 3 * span * groups), bf16),
        scratch_shapes=[pltpu.VMEM((SEQ_LEN, SEQ_LEN), bf16)] * 2,
        compiler_params=pltpu.CompilerParams(vmem_limit_bytes=48 * 1024 * 1024),
        cost_estimate=pl.CostEstimate(
            flops=groups * heads * 20 * SEQ_LEN * SEQ_LEN * HEAD_DIM,
            bytes_accessed=groups * SEQ_LEN * span * 16,
            transcendentals=groups * heads * SEQ_LEN * SEQ_LEN,
        ),
        name="attend_back",
    )(qkv, grad, log_total, docs_row, docs_col)


class Place:
    def __init__(self, mesh, own_rows):
        self.own_rows = own_rows
        self.rows = mesh.shape["row"]
        self.cols = mesh.shape["col"]
        self.a = self.cols // 2
        self.b = self.cols // 4
        self.rest = []
        mask = 1
        while mask < self.b:
            self.rest.append(mask)
            mask *= 2
        self.row = lax.axis_index("row")
        self.col = lax.axis_index("col")
        order = [0]
        for mask in self.rest:
            order = order + [item ^ mask for item in order]
        self.order = order

    def bit(self, mask):
        return (self.col // mask) % 2

    def swap(self, value, mask):
        return lax.ppermute(value, "col", [(i, i ^ mask) for i in range(self.cols)])

    def shift(self, value):
        return lax.ppermute(value, "row", [(i, (i + 1) % self.rows) for i in range(self.rows)])

    def on(self, lane, value, mask):
        if lane is None:
            return self.swap(value, mask)
        return lane.send(lambda item: self.swap(item, mask), value)

    def tokens_send(self, value, mask, lane, inner=1):
        width = value.shape[-1]
        split = value.reshape(-1, 2, inner * self.own_rows, width)
        bit = self.bit(mask)
        mine = lax.dynamic_index_in_dim(split, bit, 1, keepdims=False).reshape(-1, width)
        sent = lax.dynamic_index_in_dim(split, 1 - bit, 1, keepdims=False).reshape(-1, width)
        return (mine, self.on(lane, sent, mask))

    def tokens_merge(self, mine, got, mask, groups=1):
        part = mine.shape[-1] // groups
        return jnp.concatenate(
            [
                self.ordered(
                    mine[:, i * part : (i + 1) * part], got[:, i * part : (i + 1) * part], mask, 1
                )
                for i in range(groups)
            ],
            axis=1,
        )

    def features_send(self, value, mask, lane, groups=1):
        width = value.shape[2] // (2 * groups)
        bit = self.bit(mask)

        def pick(side):
            return jnp.concatenate(
                [
                    lax.dynamic_slice_in_dim(value, (2 * i + side) * width, width, 2)
                    for i in range(groups)
                ],
                axis=2,
            )

        return (pick(bit), self.on(lane, pick(1 - bit), mask))

    def features_merge(self, mine, got, mask, axis):
        value = self.ordered(jnp.expand_dims(mine, axis), jnp.expand_dims(got, axis), mask, axis)
        return value.reshape(-1, *mine.shape[1:])

    def ordered(self, mine, got, mask, axis):
        low = self.bit(mask) == 0
        return jnp.concatenate(
            [jnp.where(low, mine, got), jnp.where(low, got, mine)], axis=axis
        )

    def all_features(self, value, lane_of):
        for mask in self.rest + [self.b, self.a]:
            value = self.ordered(value, self.on(lane_of(mask), value, mask), mask, 1)
        return value


    def blocks(self, value, pieces, axis):
        size = pieces[0].shape[axis] // self.rows
        found = []
        for step in range(self.rows):
            at = ((self.row - 1 - step + 2 * self.rows) % self.rows) * size
            found.append(
                jnp.concatenate(
                    [lax.dynamic_slice_in_dim(item, at, size, axis) for item in pieces], axis=value
                )
            )
        return found

    def parts(self, sums, mask):
        width = sums.shape[1] // 2
        bit = self.bit(mask)
        return (
            lax.dynamic_slice_in_dim(sums, bit * width, width, 1),
            lax.dynamic_slice_in_dim(sums, (1 - bit) * width, width, 1),
        )

    def halve(self, sums, mask, lane):
        mine, sent = self.parts(sums, mask)
        return mine + self.on(lane, sent, mask)

    def row_sum(self, value, lane):
        mask = 1
        while mask < self.rows:
            pairs = [(i, i ^ mask) for i in range(self.rows)]
            value = value + lane.send(lambda item: lax.ppermute(item, "row", pairs), value)
            mask *= 2
        return value


def norm_forward(residual, gain, shift):
    mean = jnp.mean(residual, axis=1, keepdims=True)
    center = residual - mean
    inverse = lax.rsqrt(jnp.mean(center * center, axis=1, keepdims=True) + EPSILON)
    normed = center * inverse
    return (normed * gain + shift, normed, inverse)


def norm_backward(grad, normed, inverse, gain):
    scaled = grad * gain
    mean = jnp.mean(scaled, axis=1, keepdims=True)
    along = jnp.mean(scaled * normed, axis=1, keepdims=True)
    result = inverse * (scaled - mean - normed * along)
    return (result, jnp.sum(grad * normed, axis=0), jnp.sum(grad, axis=0))


def gelu(value):
    return jax.nn.gelu(value, approximate=True)


def gelu_slope(value):
    inner = 0.7978845608028654
    cubic = 0.044715
    square = value * value
    tangent = jnp.tanh(inner * value * (1.0 + cubic * square))
    return 0.5 * (1.0 + tangent) + 0.5 * value * (1.0 - tangent * tangent) * inner * (
        1.0 + 3.0 * cubic * square
    )


class Clock:
    def __init__(self):
        self.last = None

    def hold(self, value, *others):
        return after(value, self.last, *others)

    def run(self, work, *args):
        self.last = work(*self.hold(args))
        return self.last

    def wait(self, *results):
        self.last = (self.last, results)

    def aside(self, work, *args):
        return work(*self.hold(args))


class Lane:
    def __init__(self, clock, width=1):
        self.clock = clock
        self.width = width
        self.done = []

    def send(self, move, value):
        wait = self.done[-self.width] if len(self.done) >= self.width else None
        result = move(after(value, wait))
        self.done.append(result)
        return result


class Weights:
    def __init__(self, place, clock, ring, blocks):
        self.place, self.clock, self.ring = place, clock, ring
        self.entries = blocks
        self.own = {name: [entry[1]] for name, entry in blocks.items()}
        self.other = {name: [] for name in blocks}
        self.wholes = {}

    def exchange(self, name):
        whole, block, far, lane, axis, corner, spans = self.entries[name]
        step = len(self.other[name])
        self.other[name].append(
            lane.send(lambda value: self.place.swap(value, far), self.own[name][step])
        )

    def exchange_all(self, name):
        whole, block, far, lane, axis, corner, spans = self.entries[name]
        blocks = jnp.concatenate(self.own[name], axis=0)
        got = lane.send(lambda value: self.place.swap(value, far), blocks)
        self.other[name] = jnp.split(got, self.place.rows, axis=0)

    def step(self, name):
        self.own[name].append(self.ring.send(self.place.shift, self.own[name][-1]))

    def arrived(self, step, *names):
        self.clock.wait([self.own[name][step] for name in names])

    def put(self, name, step, side):
        place = self.place
        whole, block, far, lane, axis, corner, spans = self.entries[name]
        items = self.other if side else self.own
        at = ((place.row - step + place.rows) % place.rows) * spans[axis] + corner[axis]
        start = [0, 0]
        start[axis] = at
        start[1 - axis] = side * spans[1 - axis] + corner[1 - axis]
        if whole not in self.wholes:
            shape = [0, 0]
            shape[axis], shape[1 - axis] = place.rows * spans[axis], 2 * spans[1 - axis]
            self.wholes[whole] = jnp.full(shape, len(self.wholes), block.dtype)
        self.wholes[whole] = self.clock.run(
            lambda total, item: lax.dynamic_update_slice(total, item, start),
            self.wholes[whole],
            items[name][step],
        )


def entry(name, block, far, lane, axis):
    return {name: (name, block, far, lane, axis, (0, 0), block.shape)}


def halves(name, block, far, lane, axis):
    half = block.shape[0] // 2
    return {
        name + "0": (name, block[:half], far, lane, axis, (0, 0), block.shape),
        name + "1": (name, block[half:], far, lane, axis, (half, 0), block.shape),
    }


def join(pair):
    return jnp.concatenate(pair, axis=0)


def columns(pair, split):
    return (join([item[:, :split] for item in pair]), join([item[:, split:] for item in pair]))


class Exchange:
    def __init__(self, place, clock, lane, far):
        self.place, self.clock, self.lane, self.bit = place, clock, lane, far

    def far(self, value):
        return self.lane.send(lambda item: self.place.swap(item, self.bit), value)

    def near(self, value):
        for mask in self.place.rest:
            value = self.clock.run(
                lambda own, got: jnp.concatenate([own, got], axis=0),
                value,
                self.place.swap(self.clock.hold(value), mask),
            )
        return value

    def halved(self, terms):
        for mask in self.place.rest[::-1]:
            half = terms.shape[0] // 2
            got = self.place.swap(self.clock.hold(terms[half:]), mask)
            if mask == self.place.rest[0]:
                return (terms[:half], got)
            terms = self.clock.run(
                lambda own, more: (own.astype(f32) + more.astype(f32)).astype(bf16),
                terms[:half],
                got,
            )
        return (terms, jnp.zeros_like(terms))

    def sum_far(self, terms):
        kept, got = self.halved(terms)
        part = self.clock.run(
            lambda own, more: (own.astype(f32) + more.astype(f32)).astype(bf16), kept, got
        )
        return self.far(part)


def plus(*items):
    total = items[0].astype(f32)
    for item in items[1:]:
        total = total + item.astype(f32)
    return total


def local(
    mesh,
    tokens,
    cotangent,
    segments,
    query_weight,
    query_bias,
    key_weight,
    value_weight,
    value_bias,
    output_weight,
    output_bias,
    first_gain,
    first_shift,
    up_weight,
    up_bias,
    down_weight,
    down_bias,
    second_gain,
    second_shift,
):
    place = Place(mesh, tokens.shape[0] // mesh.shape["col"])
    clock = Clock()
    run = clock.run
    rows = place.rows
    steps = range(1, rows)
    span = query_weight.shape[1]
    hidden_span = up_weight.shape[1]
    own_rows = place.own_rows
    lane_a, lane_b, row_lane = Lane(clock), Lane(clock), Lane(clock)
    across_b = Exchange(place, clock, lane_b, place.b)
    across_a = Exchange(place, clock, lane_a, place.a)

    def on_lane(mask):
        return lane_a if mask == place.a else lane_b if mask == place.b else None

    def project(rows_in, weight, bias):
        return (dot(rows_in, weight) + bias).astype(bf16)

    def up_product(rows_in, weight, bias):
        hidden = dot(rows_in, weight) + bias
        return (hidden, gelu(hidden).astype(bf16))

    def product(rows_in, weight):
        return dot(rows_in, weight).astype(bf16)

    def norm(residual, kept, got, sent, bias, gain, shift):
        result, normed, inverse = norm_forward(plus(residual, kept, got, sent) + bias, gain, shift)
        return (result, result.astype(bf16), normed, inverse)

    w_all = jnp.concatenate([query_weight, key_weight, value_weight], axis=1)
    ring = Weights(
        place,
        clock,
        row_lane,
        {
            **entry("qkv", w_all, place.a, lane_a, 0),
            **entry("out", output_weight, place.a, lane_a, 1),
            **entry("up", up_weight, place.b, lane_b, 0),
            **halves("down", down_weight, place.b, lane_b, 1),
        },
    )

    def steps_of(*names):
        for name in names:
            ring.step(name)

    def exchanges(*names):
        for name in names:
            ring.exchange(name)

    def puts(step, side, *names):
        for name in names:
            ring.put(name, step, side)

    def merge(mask, groups=1):
        return lambda mine, got: place.tokens_merge(mine, got, mask, groups)

    def blocks(*pieces):
        return place.blocks(0, pieces, 1)

    exchanges("qkv")
    steps_of("qkv")
    value = tokens
    for mask in place.rest:
        value = run(merge(mask), *place.tokens_send(value, mask, None))
    value = place.tokens_send(value, place.b, lane_b)
    vectors = jnp.stack(
        [output_bias, first_gain, first_shift, down_bias, second_gain, second_shift]
    )
    for mask in place.rest:
        vectors = place.ordered(vectors, place.swap(vectors, mask), mask, 1)
    got, up_bias_other = lane_b.send(
        lambda items: tuple(place.swap(item, place.b) for item in items), (vectors, up_bias)
    )
    vectors = place.ordered(vectors, got, place.b, 1)
    b_up = jnp.concatenate([up_bias, up_bias_other])
    exchanges("up")
    puts(0, 0, "qkv", "out")
    masks = place.order + [item ^ place.b for item in place.order]
    docs = jnp.concatenate(
        [
            lax.dynamic_slice_in_dim(
                segments, jnp.bitwise_xor(place.col, mask) * own_rows, own_rows, 0
            )
            for mask in masks
        ]
    )
    docs = (docs[None, :], docs[:, None])
    value = run(merge(place.b), *value)
    value = place.tokens_send(value, place.a, lane_a)
    ring.arrived(1, "qkv")
    steps_of("qkv")
    puts(0, 1, "qkv")
    pair = jnp.concatenate([query_bias, jnp.zeros_like(query_bias), value_bias])
    pair_other, got = lane_a.send(
        lambda items: tuple(place.swap(item, place.a) for item in items), (pair, vectors)
    )
    b_qkv = jnp.concatenate([pair, pair_other])
    vectors = place.ordered(vectors, got, place.a, 1)
    b_out, gain1, shift1, b_down, gain2, shift2 = (vectors[i] for i in range(6))
    puts(1, 0, "qkv")
    for step in range(1, rows):
        exchanges("qkv")
        if step < rows - 2:
            steps_of("qkv")
    state_low = run(merge(place.a), *value)
    state = state_low.astype(f32)
    far = across_b.far(state_low)
    exchanges("down0", "down1")
    own = across_b.near(state_low)
    clock.wait(b_qkv, b_up, vectors)
    for step in range(2, rows):
        ring.arrived(step, "qkv")
        if step == rows - 1:
            steps_of("out")
        puts(step, 0, "qkv")
        puts(step - 1, 1, "qkv")
    for step in range(1, rows):
        ring.arrived(step, "out")
        steps_of("out" if step < rows - 1 else "up")
        puts(step, 0, "out")
    ring.exchange_all("out")
    other = across_b.near(far)
    puts(0, 0, "up")
    puts(0, 1, "up")
    puts(rows - 1, 1, "qkv")
    w_qkv = ring.wholes["qkv"]
    clock.wait(ring.other["down0"][0])
    qkv_own = run(project, own, w_qkv, b_qkv)
    ring.arrived(1, "up")
    steps_of("up")
    clock.wait(ring.other["down1"][0])
    exchanges("up")
    qkv_other = run(project, other, w_qkv, b_qkv)
    qkv = run(lambda *items: join(items), qkv_own, qkv_other)
    puts(1, 0, "up")
    ring.arrived(2, "up")
    steps_of("up" if rows > 3 else "down0")
    mixed, log_total = run(lambda item: attend(item, span, *docs), qkv)
    for step in range(rows):
        puts(step, 1, "out")
    w_out = ring.wholes["out"]
    half = mixed.shape[0] // 2
    terms = run(product, mixed[half:], w_out)
    sent = across_b.sum_far(terms)
    puts(1, 1, "up")
    terms = run(product, mixed[:half], w_out)
    sums = across_b.halved(terms)
    exchanges("up")
    puts(2, 0, "up")
    for step in range(3, rows):
        ring.arrived(step, "up")
        steps_of("up" if step < rows - 1 else "down0")
        exchanges("up")
        puts(step, 0, "up")
    puts(0, 0, "down0", "down1")
    puts(0, 1, "down0", "down1")
    far_half = ring.entries["down1"]
    corner = (far_half[5][0] + far_half[6][0], 0)
    ring.entries["more"] = (*far_half[:5], corner, far_half[6])
    ring.own["more"] = ring.other["down1"]
    queue = ["down0"] * (rows - 2) + ["down1", "more"] * (rows - 1)
    first, first_low, normed1, inverse1 = run(norm, state, *sums, sent, b_out, gain1, shift1)
    far = across_a.far(first_low)
    ring.arrived(1, "down0")
    steps_of(queue.pop(0))
    exchanges("down0")
    own_first = across_a.near(first_low)
    puts(2, 1, "up")
    puts(1, 0, "down0")
    ring.arrived(2, "down0")
    steps_of(queue.pop(0))
    exchanges("down0")
    puts(2, 0, "down0")
    other_first = across_a.near(far)
    for step in range(3, rows):
        ring.arrived(step, "down0")
        steps_of(queue.pop(0))
        exchanges("down0")
        puts(step, 1, "up")
        puts(step, 0, "down0")
    w_up = ring.wholes["up"]
    ring.arrived(1, "down1")
    steps_of(queue.pop(0))
    hidden_own, active_own = run(up_product, own_first, w_up, b_up)
    ring.arrived(1, "more")
    steps_of(queue.pop(0))
    hidden_other, active_other = run(up_product, other_first, w_up, b_up)
    ring.arrived(2, "down1")
    steps_of(queue.pop(0))
    puts(1, 1, "down0")
    puts(1, 0, "down1", "more")
    token_pieces = run(blocks, own, other)
    ring.arrived(2, "more")
    if queue:
        steps_of(queue.pop(0))
    puts(2, 1, "down0")
    puts(2, 0, "down1", "more")
    for step in range(3, rows):
        ring.arrived(step, "down1")
        if queue:
            steps_of(queue.pop(0))
        puts(step, 1, "down0")
        puts(step, 0, "down1")
        ring.arrived(step, "more")
        if queue:
            steps_of(queue.pop(0))
        if step < rows - 1:
            puts(step, 0, "more")
    first_pieces = run(blocks, own_first, other_first)
    active_sides = run(lambda *items: columns(items, hidden_span), active_own, active_other)
    if rows > 3:
        puts(rows - 1, 0, "more")
    w_down = ring.wholes["down"]
    terms_other = run(product, active_other, w_down)
    sent = across_a.sum_far(terms_other)
    terms_own = run(product, active_own, w_down)
    sums = across_a.halved(terms_own)
    kept_attention = [(token_pieces, qkv, mixed, log_total, normed1, inverse1)]
    state, state_low, normed2, inverse2 = run(
        norm, first, *sums, sent, b_down, gain2, shift2
    )
    kept_feed = [(first_pieces, (hidden_own, hidden_other), active_sides, normed2, inverse2)]

    grad = cotangent
    for mask in place.rest:
        grad = clock.aside(merge(mask), *place.tokens_send(grad, mask, None))
    for depth in range(1, LAYERS):
        far = across_b.far(state_low)
        own = across_b.near(state_low)
        qkv_own = run(project, own, w_qkv, b_qkv)
        other = across_b.near(far)
        qkv_other = run(project, other, w_qkv, b_qkv)
        qkv = run(lambda *items: join(items), qkv_own, qkv_other)
        if depth == 1:
            grad = place.tokens_send(grad, place.a, lane_a, 2)
        mixed, log_total = run(lambda item: attend(item, span, *docs), qkv)
        terms = run(product, mixed[half:], w_out)
        sent = across_b.sum_far(terms)
        terms = run(product, mixed[:half], w_out)
        sums = across_b.halved(terms)
        token_pieces = run(blocks, own, other)
        if depth == 1:
            grad = run(merge(place.a), *grad)
        first, first_low, normed1, inverse1 = run(norm, state, *sums, sent, b_out, gain1, shift1)
        kept_attention.append((token_pieces, qkv, mixed, log_total, normed1, inverse1))
        far = across_a.far(first_low)
        own = across_a.near(first_low)
        if depth == 1:
            grad = place.tokens_send(grad, place.b, lane_b)
        hidden_own, active_own = run(up_product, own, w_up, b_up)
        terms_own = run(product, active_own, w_down)
        own_sums = across_a.halved(terms_own)
        other = across_a.near(far)
        hidden_other, active_other = run(up_product, other, w_up, b_up)
        terms_other = run(product, active_other, w_down)
        sent = across_a.sum_far(terms_other)
        if depth == 1:
            grad = run(merge(place.b, 2), *grad)
        first_pieces = run(blocks, own, other)
        active_sides = run(lambda *items: columns(items, hidden_span), active_own, active_other)
        state, state_low, normed2, inverse2 = run(
            norm, first, *own_sums, sent, b_down, gain2, shift2
        )
        kept_feed.append(
            (first_pieces, (hidden_own, hidden_other), active_sides, normed2, inverse2)
        )
    output = state_low[None]

    def gelu_back(rows_in, weight, hidden):
        return (dot_t(rows_in, weight) * gelu_slope(hidden)).astype(bf16)

    def product_t(rows_in, weight):
        return dot_t(rows_in, weight).astype(bf16)

    def norm_back(grads, normed, inverse, gain):
        result, gain_grad, shift_grad = norm_backward(plus(*grads), normed, inverse, gain)
        low = result.astype(bf16)
        return (result, low, jnp.stack([jnp.sum(low, axis=0, dtype=f32), gain_grad, shift_grad]))

    def sum_rows(*items):
        return jnp.concatenate([jnp.sum(item, axis=0, dtype=f32) for item in items])

    class Share:
        def __init__(self, name, left, right, lane, far):
            self.name, self.left, self.right = name, left, right
            self.lane, self.far = lane, far
            self.before = held.get(name)
            self.got = []
            self.total = None
            self.step = 0

        def keep(self):
            left, right = clock.hold((self.left, self.right))
            clock.last = [
                [dot_g(left[side][step], right[side][step]) for step in range(rows)]
                for side in (0, 1)
            ]
            held[self.name] = clock.last

        def other(self):
            self.sent = []
            for step in range(rows):
                left, right = clock.hold((self.left[1][step], self.right[1][step]))
                clock.last = (dot_g(left, right) + self.before[1][step]).astype(bf16)
                self.sent.append(clock.last)

        def send(self, count=1):
            for step in range(count):
                self.got.append(
                    self.lane.send(
                        lambda item: place.swap(item, self.far), self.sent[len(self.got)]
                    )
                )

        def send_all(self):
            got = self.lane.send(
                lambda item: place.swap(item, self.far), jnp.concatenate(self.sent, axis=0)
            )
            self.got = jnp.split(got, rows, axis=0)

        def advance(self):
            step = self.step
            more = [self.got[step]] + ([] if self.total is None else [self.total])
            left, right, before, more = clock.hold(
                (self.left[0][step], self.right[0][step], self.before[0][step], more)
            )
            value = dot_g(left, right) + before
            for item in more:
                value = value + item.astype(f32)
            self.step += 1
            if step < rows - 1:
                value = value.astype(bf16)
            clock.last = self.result = value
            if step < rows - 1:
                self.total = row_lane.send(place.shift, value)

    held = {}
    norm_sums, qkv_sums, hidden_sums = [], [], []
    grads = (grad,)
    for depth in reversed(range(LAYERS)):
        last = depth == 0
        token_pieces, qkv, mixed, log_total, normed1, inverse1 = kept_attention[depth]
        first_pieces, hiddens, (active_own, active_other), normed2, inverse2 = kept_feed[depth]
        dr2, dsecond, sums2 = run(norm_back, grads, normed2, inverse2, gain2)
        far = across_a.far(dsecond)
        second_own = across_a.near(dsecond)
        if not last:
            output = place.features_send(output, place.b, lane_b, 2)
        dhid_own = run(gelu_back, second_own, w_down, hiddens[0])
        terms_own = run(product_t, dhid_own, w_up)
        own_sums = across_a.halved(terms_own)
        second_other = across_a.near(far)

        def down_share():
            pieces = run(blocks, second_own, second_other)
            return Share(
                "down",
                ([active_own] * rows, [active_other] * rows),
                (pieces, pieces),
                lane_b,
                place.b,
            )

        if last:
            down = down_share()
            down.other()
            down.send(3)
        else:
            output = run(lambda *items: place.features_merge(*items, place.b, 1), *output)
        dhid_other = run(gelu_back, second_other, w_down, hiddens[1])
        if last:
            clock.wait(down.got[0])
        terms_other = run(product_t, dhid_other, w_up)
        sent = across_a.sum_far(terms_other)
        if last:
            down.advance()
        dhid_left, dhid_right = run(lambda *items: columns(items, hidden_span), dhid_own, dhid_other)
        up = Share(
            "up",
            (first_pieces, first_pieces),
            ([dhid_left] * rows, [dhid_right] * rows),
            lane_b,
            place.b,
        )
        if last:
            up.other()
            hidden_total = hidden_sums[0] + clock.aside(sum_rows, dhid_left, dhid_right)
        else:
            down = down_share()
            down.keep()
        dr1, dbranch, sums1 = run(norm_back, (dr2, *own_sums, sent), normed1, inverse1, gain1)
        norm_sums.append(jnp.concatenate([sums1, sums2], axis=0))
        far = across_b.far(dbranch)
        branch_own = across_b.near(dbranch)
        dmixed_own = run(product_t, branch_own, w_out)
        if last:
            token_sums = place.halve(sum(norm_sums), place.a, lane_a)
            down.advance()
            down.send(rows - 3)
            mine, away = place.parts(token_sums, place.b)
            more = lane_b.send(
                lambda items: tuple(place.swap(item, place.b) for item in items),
                (away, hidden_total[hidden_span:]),
            )
            token_sums = mine + more[0]
            hidden_total = hidden_total[:hidden_span] + more[1]
            for mask in place.rest[::-1]:
                token_sums = place.halve(token_sums, mask, None)
        else:
            output = place.features_send(output, place.a, lane_a)
            up.keep()
            hidden_sums.append(clock.aside(sum_rows, dhid_left, dhid_right))
        branch_other = across_b.near(far)
        dmixed_other = run(product_t, branch_other, w_out)
        dmixed = run(lambda *items: join(items), dmixed_own, dmixed_other)
        pieces = run(blocks, branch_own, branch_other)
        out = Share(
            "out",
            ([mixed[:, :span]] * rows, [mixed[:, span:]] * rows),
            (pieces, pieces),
            lane_a,
            place.a,
        )
        if last:
            out.other()
            out.send_all()
            down.advance()
        else:
            output = run(lambda *items: place.features_merge(*items, place.a, 0), *output)
        dqkv = run(lambda *items: attend_back(*items, log_total, span, *docs), qkv, dmixed)
        qkv_sums.append(clock.aside(sum_rows, dqkv))
        if last:
            up.send(2)
            while down.step < rows:
                down.advance()
            up.advance()
        terms_other = run(product_t, dqkv[half:], w_qkv)
        sent = across_b.sum_far(terms_other)
        if not last:
            for mask in place.rest[::-1]:
                output = run(
                    lambda *items: place.features_merge(*items, mask, 1),
                    *place.features_send(output, mask, None),
                )
        both = Share(
            "qkv",
            (token_pieces, token_pieces),
            ([dqkv[:, : 3 * span]] * rows, [dqkv[:, 3 * span :]] * rows),
            lane_a,
            place.a,
        )
        if last:
            both.other()
            qkv_total = sum(qkv_sums)
            qkv_total = qkv_total[: 3 * span] + lane_a.send(
                lambda item: place.swap(item, place.a), qkv_total[3 * span :]
            )
            both.send(2)
            up.advance()
        terms_own = run(product_t, dqkv[:half], w_qkv)
        own_sums = across_b.halved(terms_own)
        if not last:
            out.keep()
            both.keep()
        grads = (dr1, *own_sums, sent)
    for step in range(rows):
        out.advance()
    grad = run(lambda *items: plus(*items).astype(bf16)[None], *grads)
    grad = place.features_send(grad, place.a, lane_a)
    up.send()
    both.send(rows - 2)
    both.advance()
    grad = run(lambda *items: place.features_merge(*items, place.a, 0), *grad)
    grad = place.features_send(grad, place.b, lane_b)
    up.send(rows - len(up.got))
    up.advance()
    sums = place.row_sum(
        jnp.concatenate([token_sums.reshape(-1), qkv_total, hidden_total]), row_lane
    )
    both.advance()
    grad = run(lambda *items: place.features_merge(*items, place.b, 1), *grad)
    for mask in place.rest[::-1]:
        grad = run(
            lambda *items: place.features_merge(*items, mask, 1),
            *place.features_send(grad, mask, None),
        )
    grad_tokens = grad.reshape(-1, span).astype(f32)
    output = output.reshape(-1, span)
    while up.step < rows:
        up.advance()
    while both.step < rows:
        both.advance()

    token_sums = sums[: 6 * span].reshape(6, span)
    qkv_sums = sums[6 * span : 9 * span]
    hidden_sums = sums[9 * span :]
    qkv = both.result
    return (
        output,
        grad_tokens,
        qkv[:, :span],
        qkv_sums[:span],
        qkv[:, span : 2 * span],
        qkv[:, 2 * span :],
        qkv_sums[2 * span :],
        out.result,
        token_sums[0],
        token_sums[1],
        token_sums[2],
        up.result,
        hidden_sums,
        down.result,
        token_sums[3],
        token_sums[4],
        token_sums[5],
    )


def solution(mesh):
    both, col, back = P("row", "col"), P("col"), P("col", "row")
    return jax.shard_map(
        functools.partial(local, mesh),
        mesh=mesh,
        in_specs=(
            both, both, P("row"), both, col, both, both, col, back, col, col, col, both, col, back,
            col, col, col,
        ),
        out_specs=(
            both, both, both, col, both, both, col, back, col, col, col, both, col, back, col, col,
            col,
        ),
        check_vma=False,
    )
```

```python
import functools

import jax
import jax.numpy as jnp
from jax import lax
from jax.experimental import pallas as pl
from jax.experimental.pallas import tpu as pltpu
from jax.sharding import PartitionSpec as P

HEAD_DIM = 128
LAYERS = 2
SEQ_LEN = 1024

EPSILON = 1e-06
MASKED = -1e30
SCALE = HEAD_DIM ** (-0.5)

bf16 = jnp.bfloat16
f32 = jnp.float32


def dot(left, right):
    return lax.dot_general(left, right, (((1,), (0,)), ((), ())), preferred_element_type=f32)


def dot_t(left, right):
    return lax.dot_general(left, right, (((1,), (1,)), ((), ())), preferred_element_type=f32)


def dot_g(left, right):
    return lax.dot_general(left, right, (((0,), (0,)), ((), ())), preferred_element_type=f32)


def after(value, *others):
    others = [item for item in others if item is not None]
    if not others:
        return value
    return lax.optimization_barrier((value, others))[0]


def attend_kernel(qkv_ref, docs_row_ref, docs_col_ref, mixed_ref, log_ref):
    step = 256
    span = mixed_ref.shape[1]
    key_docs = docs_col_ref[...]
    for head in range(span // HEAD_DIM):
        low = head * HEAD_DIM
        keys = qkv_ref[:, span + low : span + low + HEAD_DIM]
        values_t = qkv_ref[:, 2 * span + low : 2 * span + low + HEAD_DIM].T
        for start in range(0, SEQ_LEN, step):
            query = qkv_ref[start : start + step, low : low + HEAD_DIM]
            scores = dot_t(keys, query) * SCALE
            allowed = key_docs == docs_row_ref[:, start : start + step]
            scores = jnp.where(allowed, scores, MASKED)
            peak = jnp.max(scores, axis=0, keepdims=True)
            weight = jnp.exp(scores - peak)
            total = jnp.sum(weight, axis=0, keepdims=True)
            mixed_t = dot(values_t, weight.astype(bf16)) * (1.0 / total)
            mixed_ref[start : start + step, low : low + HEAD_DIM] = mixed_t.T.astype(bf16)
            log_ref[head, :, start : start + step] = peak + jnp.log(total)


def attend(qkv, span, docs_row, docs_col):
    groups = qkv.shape[1] // (3 * span)
    heads = span // HEAD_DIM
    return pl.pallas_call(
        attend_kernel,
        grid=(groups,),
        in_specs=[
            pl.BlockSpec((SEQ_LEN, 3 * span), lambda g: (0, g)),
            pl.BlockSpec((1, SEQ_LEN), lambda g: (0, 0)),
            pl.BlockSpec((SEQ_LEN, 1), lambda g: (0, 0)),
        ],
        out_specs=[
            pl.BlockSpec((SEQ_LEN, span), lambda g: (0, g)),
            pl.BlockSpec((heads, 1, SEQ_LEN), lambda g: (g, 0, 0)),
        ],
        out_shape=[
            jax.ShapeDtypeStruct((SEQ_LEN, span * groups), bf16),
            jax.ShapeDtypeStruct((heads * groups, 1, SEQ_LEN), f32),
        ],
        compiler_params=pltpu.CompilerParams(vmem_limit_bytes=48 * 1024 * 1024),
        cost_estimate=pl.CostEstimate(
            flops=groups * heads * 8 * SEQ_LEN * SEQ_LEN * HEAD_DIM,
            bytes_accessed=groups * SEQ_LEN * span * 8,
            transcendentals=groups * heads * SEQ_LEN * SEQ_LEN,
        ),
        name="attend",
    )(qkv, docs_row, docs_col)


def attend_back_kernel(
    qkv_ref, grad_ref, log_ref, docs_row_ref, docs_col_ref, out_ref, probs_ref, dscores_ref
):
    step = 256
    span = grad_ref.shape[1]
    key_docs = docs_col_ref[...]
    for head in range(span // HEAD_DIM):
        low = head * HEAD_DIM
        own = slice(low, low + HEAD_DIM)
        keys = qkv_ref[:, span + low : span + low + HEAD_DIM]
        values = qkv_ref[:, 2 * span + low : 2 * span + low + HEAD_DIM]
        for start in range(0, SEQ_LEN, step):
            at = slice(start, start + step)
            scores = dot_t(keys, qkv_ref[at, own]) * SCALE
            allowed = key_docs == docs_row_ref[:, at]
            probs = jnp.exp(jnp.where(allowed, scores, MASKED) - log_ref[head, :, at])
            dprobs = dot_t(values, grad_ref[at, own])
            along = jnp.sum(dprobs * probs, axis=0, keepdims=True)
            probs_ref[:, at] = probs.astype(bf16)
            dscores_ref[:, at] = (probs * (dprobs - along)).astype(bf16)
        dscores = dscores_ref[...]
        out_ref[:, own] = (dot(keys.T, dscores) * SCALE).T.astype(bf16)
        out_ref[:, span + low : span + low + HEAD_DIM] = (
            dot(dscores, qkv_ref[:, own]) * SCALE
        ).astype(bf16)
        out_ref[:, 2 * span + low : 2 * span + low + HEAD_DIM] = dot(
            probs_ref[...], grad_ref[:, own]
        ).astype(bf16)


def attend_back(qkv, grad, log_total, span, docs_row, docs_col):
    groups = qkv.shape[1] // (3 * span)
    heads = span // HEAD_DIM
    return pl.pallas_call(
        attend_back_kernel,
        grid=(groups,),
        in_specs=[
            pl.BlockSpec((SEQ_LEN, 3 * span), lambda g: (0, g)),
            pl.BlockSpec((SEQ_LEN, span), lambda g: (0, g)),
            pl.BlockSpec((heads, 1, SEQ_LEN), lambda g: (g, 0, 0)),
            pl.BlockSpec((1, SEQ_LEN), lambda g: (0, 0)),
            pl.BlockSpec((SEQ_LEN, 1), lambda g: (0, 0)),
        ],
        out_specs=pl.BlockSpec((SEQ_LEN, 3 * span), lambda g: (0, g)),
        out_shape=jax.ShapeDtypeStruct((SEQ_LEN, 3 * span * groups), bf16),
        scratch_shapes=[pltpu.VMEM((SEQ_LEN, SEQ_LEN), bf16)] * 2,
        compiler_params=pltpu.CompilerParams(vmem_limit_bytes=48 * 1024 * 1024),
        cost_estimate=pl.CostEstimate(
            flops=groups * heads * 20 * SEQ_LEN * SEQ_LEN * HEAD_DIM,
            bytes_accessed=groups * SEQ_LEN * span * 16,
            transcendentals=groups * heads * SEQ_LEN * SEQ_LEN,
        ),
        name="attend_back",
    )(qkv, grad, log_total, docs_row, docs_col)


class Place:
    def __init__(self, mesh, own_rows):
        self.own_rows = own_rows
        self.rows = mesh.shape["row"]
        self.cols = mesh.shape["col"]
        self.a = self.cols // 2
        self.b = self.cols // 4
        self.rest = []
        mask = 1
        while mask < self.b:
            self.rest.append(mask)
            mask *= 2
        self.row = lax.axis_index("row")
        self.col = lax.axis_index("col")
        order = [0]
        for mask in self.rest:
            order = order + [item ^ mask for item in order]
        self.order = order

    def bit(self, mask):
        return (self.col // mask) % 2

    def swap(self, value, mask):
        return lax.ppermute(value, "col", [(i, i ^ mask) for i in range(self.cols)])

    def shift(self, value):
        return lax.ppermute(value, "row", [(i, (i + 1) % self.rows) for i in range(self.rows)])

    def on(self, lane, value, mask):
        if lane is None:
            return self.swap(value, mask)
        return lane.send(lambda item: self.swap(item, mask), value)

    def tokens_send(self, value, mask, lane, inner=1):
        width = value.shape[-1]
        split = value.reshape(-1, 2, inner * self.own_rows, width)
        bit = self.bit(mask)
        mine = lax.dynamic_index_in_dim(split, bit, 1, keepdims=False).reshape(-1, width)
        sent = lax.dynamic_index_in_dim(split, 1 - bit, 1, keepdims=False).reshape(-1, width)
        return (mine, self.on(lane, sent, mask))

    def tokens_merge(self, mine, got, mask, groups=1):
        part = mine.shape[-1] // groups
        return jnp.concatenate(
            [
                self.ordered(
                    mine[:, i * part : (i + 1) * part], got[:, i * part : (i + 1) * part], mask, 1
                )
                for i in range(groups)
            ],
            axis=1,
        )

    def features_send(self, value, mask, lane, groups=1):
        width = value.shape[2] // (2 * groups)
        bit = self.bit(mask)

        def pick(side):
            return jnp.concatenate(
                [
                    lax.dynamic_slice_in_dim(value, (2 * i + side) * width, width, 2)
                    for i in range(groups)
                ],
                axis=2,
            )

        return (pick(bit), self.on(lane, pick(1 - bit), mask))

    def features_merge(self, mine, got, mask, axis):
        value = self.ordered(jnp.expand_dims(mine, axis), jnp.expand_dims(got, axis), mask, axis)
        return value.reshape(-1, *mine.shape[1:])

    def ordered(self, mine, got, mask, axis):
        low = self.bit(mask) == 0
        return jnp.concatenate(
            [jnp.where(low, mine, got), jnp.where(low, got, mine)], axis=axis
        )

    def all_features(self, value, lane_of):
        for mask in self.rest + [self.b, self.a]:
            value = self.ordered(value, self.on(lane_of(mask), value, mask), mask, 1)
        return value


    def blocks(self, value, pieces, axis):
        size = pieces[0].shape[axis] // self.rows
        found = []
        for step in range(self.rows):
            at = ((self.row - 1 - step + 2 * self.rows) % self.rows) * size
            found.append(
                jnp.concatenate(
                    [lax.dynamic_slice_in_dim(item, at, size, axis) for item in pieces], axis=value
                )
            )
        return found

    def parts(self, sums, mask):
        width = sums.shape[1] // 2
        bit = self.bit(mask)
        return (
            lax.dynamic_slice_in_dim(sums, bit * width, width, 1),
            lax.dynamic_slice_in_dim(sums, (1 - bit) * width, width, 1),
        )

    def halve(self, sums, mask, lane):
        mine, sent = self.parts(sums, mask)
        return mine + self.on(lane, sent, mask)

    def row_sum(self, value, lane):
        mask = 1
        while mask < self.rows:
            pairs = [(i, i ^ mask) for i in range(self.rows)]
            value = value + lane.send(lambda item: lax.ppermute(item, "row", pairs), value)
            mask *= 2
        return value


def norm_forward(residual, gain, shift):
    mean = jnp.mean(residual, axis=1, keepdims=True)
    center = residual - mean
    inverse = lax.rsqrt(jnp.mean(center * center, axis=1, keepdims=True) + EPSILON)
    normed = center * inverse
    return (normed * gain + shift, normed, inverse)


def norm_backward(grad, normed, inverse, gain):
    scaled = grad * gain
    mean = jnp.mean(scaled, axis=1, keepdims=True)
    along = jnp.mean(scaled * normed, axis=1, keepdims=True)
    result = inverse * (scaled - mean - normed * along)
    return (result, jnp.sum(grad * normed, axis=0), jnp.sum(grad, axis=0))


def gelu(value):
    return jax.nn.gelu(value, approximate=True)


def gelu_slope(value):
    inner = 0.7978845608028654
    cubic = 0.044715
    square = value * value
    tangent = jnp.tanh(inner * value * (1.0 + cubic * square))
    return 0.5 * (1.0 + tangent) + 0.5 * value * (1.0 - tangent * tangent) * inner * (
        1.0 + 3.0 * cubic * square
    )


class Clock:
    def __init__(self):
        self.last = None

    def hold(self, value, *others):
        return after(value, self.last, *others)

    def run(self, work, *args):
        self.last = work(*self.hold(args))
        return self.last

    def wait(self, *results):
        self.last = (self.last, results)

    def aside(self, work, *args):
        return work(*self.hold(args))


class Lane:
    def __init__(self, clock, width=1):
        self.clock = clock
        self.width = width
        self.done = []

    def send(self, move, value):
        wait = self.done[-self.width] if len(self.done) >= self.width else None
        result = move(after(value, wait))
        self.done.append(result)
        return result


class Weights:
    def __init__(self, place, clock, ring, blocks):
        self.place, self.clock, self.ring = place, clock, ring
        self.entries = blocks
        self.own = {name: [entry[1]] for name, entry in blocks.items()}
        self.other = {name: [] for name in blocks}
        self.wholes = {}

    def exchange(self, name):
        whole, block, far, lane, axis, corner, spans = self.entries[name]
        step = len(self.other[name])
        self.other[name].append(
            lane.send(lambda value: self.place.swap(value, far), self.own[name][step])
        )

    def exchange_all(self, name):
        whole, block, far, lane, axis, corner, spans = self.entries[name]
        blocks = jnp.concatenate(self.own[name], axis=0)
        got = lane.send(lambda value: self.place.swap(value, far), blocks)
        self.other[name] = jnp.split(got, self.place.rows, axis=0)

    def step(self, name):
        self.own[name].append(self.ring.send(self.place.shift, self.own[name][-1]))

    def arrived(self, step, *names):
        self.clock.wait([self.own[name][step] for name in names])

    def put(self, name, step, side):
        place = self.place
        whole, block, far, lane, axis, corner, spans = self.entries[name]
        items = self.other if side else self.own
        at = ((place.row - step + place.rows) % place.rows) * spans[axis] + corner[axis]
        start = [0, 0]
        start[axis] = at
        start[1 - axis] = side * spans[1 - axis] + corner[1 - axis]
        if whole not in self.wholes:
            shape = [0, 0]
            shape[axis], shape[1 - axis] = place.rows * spans[axis], 2 * spans[1 - axis]
            self.wholes[whole] = jnp.full(shape, len(self.wholes), block.dtype)
        self.wholes[whole] = self.clock.run(
            lambda total, item: lax.dynamic_update_slice(total, item, start),
            self.wholes[whole],
            items[name][step],
        )


def entry(name, block, far, lane, axis):
    return {name: (name, block, far, lane, axis, (0, 0), block.shape)}


def halves(name, block, far, lane, axis):
    half = block.shape[0] // 2
    return {
        name + "0": (name, block[:half], far, lane, axis, (0, 0), block.shape),
        name + "1": (name, block[half:], far, lane, axis, (half, 0), block.shape),
    }


def join(pair):
    return jnp.concatenate(pair, axis=0)


def columns(pair, split):
    return (join([item[:, :split] for item in pair]), join([item[:, split:] for item in pair]))


class Exchange:
    def __init__(self, place, clock, lane, far):
        self.place, self.clock, self.lane, self.bit = place, clock, lane, far

    def far(self, value):
        return self.lane.send(lambda item: self.place.swap(item, self.bit), value)

    def near(self, value):
        for mask in self.place.rest:
            value = self.clock.run(
                lambda own, got: jnp.concatenate([own, got], axis=0),
                value,
                self.place.swap(self.clock.hold(value), mask),
            )
        return value

    def halved(self, terms):
        for mask in self.place.rest[::-1]:
            half = terms.shape[0] // 2
            got = self.place.swap(self.clock.hold(terms[half:]), mask)
            if mask == self.place.rest[0]:
                return (terms[:half], got)
            terms = self.clock.run(
                lambda own, more: (own.astype(f32) + more.astype(f32)).astype(bf16),
                terms[:half],
                got,
            )
        return (terms, jnp.zeros_like(terms))

    def sum_far(self, terms, meanwhile=None):
        kept, got = self.halved(terms)
        if meanwhile is not None:
            meanwhile()
        part = self.clock.run(
            lambda own, more: (own.astype(f32) + more.astype(f32)).astype(bf16), kept, got
        )
        return self.far(part)


def plus(*items):
    total = items[0].astype(f32)
    for item in items[1:]:
        total = total + item.astype(f32)
    return total


def local(
    mesh,
    tokens,
    cotangent,
    segments,
    query_weight,
    query_bias,
    key_weight,
    value_weight,
    value_bias,
    output_weight,
    output_bias,
    first_gain,
    first_shift,
    up_weight,
    up_bias,
    down_weight,
    down_bias,
    second_gain,
    second_shift,
):
    place = Place(mesh, tokens.shape[0] // mesh.shape["col"])
    clock = Clock()
    run = clock.run
    rows = place.rows
    steps = range(1, rows)
    span = query_weight.shape[1]
    hidden_span = up_weight.shape[1]
    own_rows = place.own_rows
    lane_a, lane_b, row_lane = Lane(clock), Lane(clock), Lane(clock)
    across_b = Exchange(place, clock, lane_b, place.b)
    across_a = Exchange(place, clock, lane_a, place.a)

    def on_lane(mask):
        return lane_a if mask == place.a else lane_b if mask == place.b else None

    def project(rows_in, weight, bias):
        return (dot(rows_in, weight) + bias).astype(bf16)

    def up_product(rows_in, weight, bias):
        hidden = dot(rows_in, weight) + bias
        return (hidden, gelu(hidden).astype(bf16))

    def product(rows_in, weight):
        return dot(rows_in, weight).astype(bf16)

    def norm(residual, kept, got, sent, bias, gain, shift):
        result, normed, inverse = norm_forward(plus(residual, kept, got, sent) + bias, gain, shift)
        return (result, result.astype(bf16), normed, inverse)

    w_all = jnp.concatenate([query_weight, key_weight, value_weight], axis=1)
    ring = Weights(
        place,
        clock,
        row_lane,
        {
            **entry("qkv", w_all, place.a, lane_a, 0),
            **entry("out", output_weight, place.a, lane_a, 1),
            **entry("up", up_weight, place.b, lane_b, 0),
            **halves("down", down_weight, place.b, lane_b, 1),
        },
    )

    def steps_of(*names):
        for name in names:
            ring.step(name)

    def exchanges(*names):
        for name in names:
            ring.exchange(name)

    def puts(step, side, *names):
        for name in names:
            ring.put(name, step, side)

    def merge(mask, groups=1):
        return lambda mine, got: place.tokens_merge(mine, got, mask, groups)

    def blocks(*pieces):
        return place.blocks(0, pieces, 1)

    exchanges("qkv")
    steps_of("qkv")
    value = tokens
    for mask in place.rest:
        value = run(merge(mask), *place.tokens_send(value, mask, None))
    value = place.tokens_send(value, place.b, lane_b)
    vectors = jnp.stack(
        [output_bias, first_gain, first_shift, down_bias, second_gain, second_shift]
    )
    for mask in place.rest:
        vectors = place.ordered(vectors, place.swap(vectors, mask), mask, 1)
    got, up_bias_other = lane_b.send(
        lambda items: tuple(place.swap(item, place.b) for item in items), (vectors, up_bias)
    )
    vectors = place.ordered(vectors, got, place.b, 1)
    b_up = jnp.concatenate([up_bias, up_bias_other])
    exchanges("up")
    puts(0, 0, "qkv", "out")
    masks = place.order + [item ^ place.b for item in place.order]
    docs = jnp.concatenate(
        [
            lax.dynamic_slice_in_dim(
                segments, jnp.bitwise_xor(place.col, mask) * own_rows, own_rows, 0
            )
            for mask in masks
        ]
    )
    docs = (docs[None, :], docs[:, None])
    value = run(merge(place.b), *value)
    value = place.tokens_send(value, place.a, lane_a)
    ring.arrived(1, "qkv")
    steps_of("qkv")
    puts(0, 1, "qkv")
    pair = jnp.concatenate([query_bias, jnp.zeros_like(query_bias), value_bias])
    pair_other, got = lane_a.send(
        lambda items: tuple(place.swap(item, place.a) for item in items), (pair, vectors)
    )
    b_qkv = jnp.concatenate([pair, pair_other])
    vectors = place.ordered(vectors, got, place.a, 1)
    b_out, gain1, shift1, b_down, gain2, shift2 = (vectors[i] for i in range(6))
    puts(1, 0, "qkv")
    for step in range(1, rows):
        exchanges("qkv")
        if step < rows - 2:
            steps_of("qkv")
    state_low = run(merge(place.a), *value)
    state = state_low.astype(f32)
    far = across_b.far(state_low)
    exchanges("down0", "down1")
    own = across_b.near(state_low)
    clock.wait(b_qkv, b_up, vectors)
    for step in range(2, rows):
        ring.arrived(step, "qkv")
        if step == rows - 1:
            steps_of("out")
        puts(step, 0, "qkv")
        puts(step - 1, 1, "qkv")
    for step in range(1, rows):
        ring.arrived(step, "out")
        steps_of("out" if step < rows - 1 else "up")
        puts(step, 0, "out")
    ring.exchange_all("out")
    other = across_b.near(far)
    puts(0, 0, "up")
    puts(0, 1, "up")
    puts(rows - 1, 1, "qkv")
    w_qkv = ring.wholes["qkv"]
    clock.wait(ring.other["down0"][0])
    qkv_own = run(project, own, w_qkv, b_qkv)
    ring.arrived(1, "up")
    steps_of("up")
    clock.wait(ring.other["down1"][0])
    exchanges("up")
    qkv_other = run(project, other, w_qkv, b_qkv)
    qkv = run(lambda *items: join(items), qkv_own, qkv_other)
    puts(1, 0, "up")
    ring.arrived(2, "up")
    steps_of("up" if rows > 3 else "down0")
    mixed, log_total = run(lambda item: attend(item, span, *docs), qkv)
    clock.wait(ring.other["up"][1])
    for step in range(rows):
        puts(step, 1, "out")
    w_out = ring.wholes["out"]
    half = mixed.shape[0] // 2
    terms_other = run(product, mixed[half:], w_out)
    terms_own = []

    def meanwhile():
        terms_own.append(run(product, mixed[:half], w_out))
        puts(1, 1, "up")

    sent = across_b.sum_far(terms_other, meanwhile)
    sums = across_b.halved(terms_own[0])
    exchanges("up")
    puts(2, 0, "up")
    for step in range(3, rows):
        ring.arrived(step, "up")
        steps_of("up" if step < rows - 1 else "down0")
        exchanges("up")
        puts(step, 0, "up")
    puts(0, 0, "down0", "down1")
    puts(0, 1, "down0", "down1")
    far_half = ring.entries["down1"]
    corner = (far_half[5][0] + far_half[6][0], 0)
    ring.entries["more"] = (*far_half[:5], corner, far_half[6])
    ring.own["more"] = ring.other["down1"]
    queue = ["down0"] * (rows - 2) + ["down1", "more"] * (rows - 1)
    first, first_low, normed1, inverse1 = run(norm, state, *sums, sent, b_out, gain1, shift1)
    far = across_a.far(first_low)
    ring.arrived(1, "down0")
    steps_of(queue.pop(0))
    exchanges("down0")
    own_first = across_a.near(first_low)
    puts(2, 1, "up")
    puts(1, 0, "down0")
    ring.arrived(2, "down0")
    steps_of(queue.pop(0))
    exchanges("down0")
    puts(2, 0, "down0")
    other_first = across_a.near(far)
    for step in range(3, rows):
        ring.arrived(step, "down0")
        steps_of(queue.pop(0))
        exchanges("down0")
        puts(step, 1, "up")
        puts(step, 0, "down0")
    w_up = ring.wholes["up"]
    ring.arrived(1, "down1")
    steps_of(queue.pop(0))
    hidden_own, active_own = run(up_product, own_first, w_up, b_up)
    ring.arrived(1, "more")
    steps_of(queue.pop(0))
    hidden_other, active_other = run(up_product, other_first, w_up, b_up)
    ring.arrived(2, "down1")
    steps_of(queue.pop(0))
    puts(1, 1, "down0")
    puts(1, 0, "down1", "more")
    token_pieces = run(blocks, own, other)
    ring.arrived(2, "more")
    if queue:
        steps_of(queue.pop(0))
    puts(2, 1, "down0")
    puts(2, 0, "down1", "more")
    for step in range(3, rows):
        ring.arrived(step, "down1")
        if queue:
            steps_of(queue.pop(0))
        puts(step, 1, "down0")
        puts(step, 0, "down1")
        ring.arrived(step, "more")
        if queue:
            steps_of(queue.pop(0))
        if step < rows - 1:
            puts(step, 0, "more")
    first_pieces = run(blocks, own_first, other_first)
    active_sides = run(lambda *items: columns(items, hidden_span), active_own, active_other)
    if rows > 3:
        puts(rows - 1, 0, "more")
    w_down = ring.wholes["down"]
    terms_other = run(product, active_other, w_down)
    sent = across_a.sum_far(terms_other)
    terms_own = run(product, active_own, w_down)
    sums = across_a.halved(terms_own)
    kept_attention = [(token_pieces, qkv, mixed, log_total, normed1, inverse1)]
    state, state_low, normed2, inverse2 = run(
        norm, first, *sums, sent, b_down, gain2, shift2
    )
    kept_feed = [(first_pieces, (hidden_own, hidden_other), active_sides, normed2, inverse2)]

    grad = cotangent
    for mask in place.rest:
        grad = clock.aside(merge(mask), *place.tokens_send(grad, mask, None))
    for depth in range(1, LAYERS):
        far = across_b.far(state_low)
        own = across_b.near(state_low)
        qkv_own = run(project, own, w_qkv, b_qkv)
        other = across_b.near(far)
        qkv_other = run(project, other, w_qkv, b_qkv)
        qkv = run(lambda *items: join(items), qkv_own, qkv_other)
        if depth == 1:
            grad = place.tokens_send(grad, place.a, lane_a, 2)
        mixed, log_total = run(lambda item: attend(item, span, *docs), qkv)
        if depth == 1:
            clock.wait(grad[1])
        terms_other = run(product, mixed[half:], w_out)
        terms_own = []
        sent = across_b.sum_far(
            terms_other, lambda: terms_own.append(run(product, mixed[:half], w_out))
        )
        sums = across_b.halved(terms_own[0])
        token_pieces = run(blocks, own, other)
        if depth == 1:
            grad = run(merge(place.a), *grad)
        first, first_low, normed1, inverse1 = run(norm, state, *sums, sent, b_out, gain1, shift1)
        kept_attention.append((token_pieces, qkv, mixed, log_total, normed1, inverse1))
        far = across_a.far(first_low)
        own = across_a.near(first_low)
        if depth == 1:
            grad = place.tokens_send(grad, place.b, lane_b)
        hidden_own, active_own = run(up_product, own, w_up, b_up)
        terms_own = run(product, active_own, w_down)
        own_sums = across_a.halved(terms_own)
        if depth == 1:
            clock.wait(grad[1])
        other = across_a.near(far)
        hidden_other, active_other = run(up_product, other, w_up, b_up)
        terms_other = run(product, active_other, w_down)
        sent = across_a.sum_far(terms_other)
        if depth == 1:
            grad = run(merge(place.b, 2), *grad)
        first_pieces = run(blocks, own, other)
        active_sides = run(lambda *items: columns(items, hidden_span), active_own, active_other)
        state, state_low, normed2, inverse2 = run(
            norm, first, *own_sums, sent, b_down, gain2, shift2
        )
        kept_feed.append(
            (first_pieces, (hidden_own, hidden_other), active_sides, normed2, inverse2)
        )
    output = state_low[None]

    def gelu_back(rows_in, weight, hidden):
        return (dot_t(rows_in, weight) * gelu_slope(hidden)).astype(bf16)

    def product_t(rows_in, weight):
        return dot_t(rows_in, weight).astype(bf16)

    def norm_back(grads, normed, inverse, gain):
        result, gain_grad, shift_grad = norm_backward(plus(*grads), normed, inverse, gain)
        low = result.astype(bf16)
        return (result, low, jnp.stack([jnp.sum(low, axis=0, dtype=f32), gain_grad, shift_grad]))

    def sum_rows(*items):
        return jnp.concatenate([jnp.sum(item, axis=0, dtype=f32) for item in items])

    class Share:
        def __init__(self, name, left, right, lane, far):
            self.name, self.left, self.right = name, left, right
            self.lane, self.far = lane, far
            self.before = held.get(name)
            self.got = []
            self.sent = []
            self.total = None
            self.step = 0

        def keep(self):
            left, right = clock.hold((self.left, self.right))
            clock.last = [
                [dot_g(left[side][step], right[side][step]) for step in range(rows)]
                for side in (0, 1)
            ]
            held[self.name] = clock.last

        def other_first(self):
            self.other(1)

        def other(self, count=None):
            for step in range(len(self.sent), rows if count is None else count):
                left, right = clock.hold((self.left[1][step], self.right[1][step]))
                clock.last = (dot_g(left, right) + self.before[1][step]).astype(bf16)
                self.sent.append(clock.last)

        def send(self, count=1):
            for step in range(count):
                self.got.append(
                    self.lane.send(
                        lambda item: place.swap(item, self.far), self.sent[len(self.got)]
                    )
                )

        def send_all(self):
            got = self.lane.send(
                lambda item: place.swap(item, self.far), jnp.concatenate(self.sent, axis=0)
            )
            self.got = jnp.split(got, rows, axis=0)

        def advance(self):
            step = self.step
            more = [self.got[step]] + ([] if self.total is None else [self.total])
            left, right, before, more = clock.hold(
                (self.left[0][step], self.right[0][step], self.before[0][step], more)
            )
            value = dot_g(left, right) + before
            for item in more:
                value = value + item.astype(f32)
            self.step += 1
            if step < rows - 1:
                value = value.astype(bf16)
            clock.last = self.result = value
            if step < rows - 1:
                self.total = row_lane.send(place.shift, value)

    held = {}
    norm_sums, qkv_sums, hidden_sums = [], [], []
    grads = (grad,)
    for depth in reversed(range(LAYERS)):
        last = depth == 0
        token_pieces, qkv, mixed, log_total, normed1, inverse1 = kept_attention[depth]
        first_pieces, hiddens, (active_own, active_other), normed2, inverse2 = kept_feed[depth]
        dr2, dsecond, sums2 = run(norm_back, grads, normed2, inverse2, gain2)
        far = across_a.far(dsecond)
        second_own = across_a.near(dsecond)
        if not last:
            output = place.features_send(output, place.b, lane_b, 2)
        dhid_own = run(gelu_back, second_own, w_down, hiddens[0])
        terms_own = run(product_t, dhid_own, w_up)
        own_sums = across_a.halved(terms_own)
        second_other = across_a.near(far)

        def down_share():
            pieces = run(blocks, second_own, second_other)
            return Share(
                "down",
                ([active_own] * rows, [active_other] * rows),
                (pieces, pieces),
                lane_b,
                place.b,
            )

        if last:
            down = down_share()
            down.other()
            down.send(3)
        dhid_other = run(gelu_back, second_other, w_down, hiddens[1])
        terms_other = run(product_t, dhid_other, w_up)
        if not last:
            clock.wait(output[1])
            output = clock.aside(lambda *items: place.features_merge(*items, place.b, 1), *output)
        sides = []
        sent = across_a.sum_far(
            terms_other,
            lambda: sides.extend(
                run(lambda *items: columns(items, hidden_span), dhid_own, dhid_other)
            ),
        )
        dhid_left, dhid_right = sides
        if last:
            down.advance()
        up = Share(
            "up",
            (first_pieces, first_pieces),
            ([dhid_left] * rows, [dhid_right] * rows),
            lane_b,
            place.b,
        )
        if last:
            up.other()
            hidden_total = hidden_sums[0] + clock.aside(sum_rows, dhid_left, dhid_right)
        else:
            down = down_share()
            down.keep()
        dr1, dbranch, sums1 = run(norm_back, (dr2, *own_sums, sent), normed1, inverse1, gain1)
        norm_sums.append(jnp.concatenate([sums1, sums2], axis=0))
        far = across_b.far(dbranch)
        branch_own = across_b.near(dbranch)
        dmixed_own = run(product_t, branch_own, w_out)
        if last:
            token_sums = place.halve(sum(norm_sums), place.a, lane_a)
            down.advance()
            down.send(rows - 3)
            up.send()
        else:
            output = place.features_send(output, place.a, lane_a)
            up.keep()
            clock.wait(output[1])
            hidden_sums.append(clock.aside(sum_rows, dhid_left, dhid_right))
        branch_other = across_b.near(far)
        dmixed_other = run(product_t, branch_other, w_out)
        dmixed = run(lambda *items: join(items), dmixed_own, dmixed_other)
        pieces = run(blocks, branch_own, branch_other)
        out = Share(
            "out",
            ([mixed[:, :span]] * rows, [mixed[:, span:]] * rows),
            (pieces, pieces),
            lane_a,
            place.a,
        )
        if last:
            out.other()
            out.send_all()
            down.advance()
            clock.wait(up.got[0])
            up.send()
        else:
            output = clock.aside(lambda *items: place.features_merge(*items, place.a, 0), *output)
        dqkv = run(lambda *items: attend_back(*items, log_total, span, *docs), qkv, dmixed)
        qkv_sums.append(clock.aside(sum_rows, dqkv))
        if last:
            clock.wait(out.got, up.got[1])
            while down.step < rows:
                down.advance()
            up.advance()
        terms_other = run(product_t, dqkv[half:], w_qkv)
        if last:
            both = Share(
                "qkv",
                (token_pieces, token_pieces),
                ([dqkv[:, : 3 * span]] * rows, [dqkv[:, 3 * span :]] * rows),
                lane_a,
                place.a,
            )
            sent = across_b.sum_far(terms_other, both.other_first)
            both.send()
        else:
            sent = across_b.sum_far(terms_other)
            for mask in place.rest[::-1]:
                output = run(
                    lambda *items: place.features_merge(*items, mask, 1),
                    *place.features_send(output, mask, None),
                )
        if not last:
            both = Share(
                "qkv",
                (token_pieces, token_pieces),
                ([dqkv[:, : 3 * span]] * rows, [dqkv[:, 3 * span :]] * rows),
                lane_a,
                place.a,
            )
        if last:
            both.other()
            both.send()
            clock.wait(sent)
            up.send()
            up.advance()
        terms_own = run(product_t, dqkv[:half], w_qkv)
        own_sums = across_b.halved(terms_own)
        if not last:
            out.keep()
            both.keep()
        grads = (dr1, *own_sums, sent)
    clock.wait(own_sums)
    for step in range(rows):
        out.advance()
    grad = run(lambda *items: plus(*items).astype(bf16)[None], *grads)
    grad = place.features_send(grad, place.a, lane_a)
    both.send(rows - 2)
    both.advance()
    grad = run(lambda *items: place.features_merge(*items, place.a, 0), *grad)
    up.send(rows - len(up.got))
    grad = place.features_send(grad, place.b, lane_b)
    up.advance()
    both.advance()
    grad = run(lambda *items: place.features_merge(*items, place.b, 1), *grad)
    for mask in place.rest[::-1]:
        grad = run(
            lambda *items: place.features_merge(*items, mask, 1),
            *place.features_send(grad, mask, None),
        )
    grad_tokens = grad.reshape(-1, span).astype(f32)
    output = output.reshape(-1, span)
    qkv_total = sum(qkv_sums)
    qkv_total = qkv_total[: 3 * span] + lane_a.send(
        lambda item: place.swap(item, place.a), qkv_total[3 * span :]
    )
    mine, away = place.parts(token_sums, place.b)
    more = lane_b.send(
        lambda items: tuple(place.swap(item, place.b) for item in items),
        (away, hidden_total[hidden_span:]),
    )
    token_sums = mine + more[0]
    hidden_total = hidden_total[:hidden_span] + more[1]
    for mask in place.rest[::-1]:
        token_sums = place.halve(token_sums, mask, None)
    while both.step < rows - 1:
        both.advance()
        if up.step < rows:
            up.advance()
    sums = place.row_sum(
        jnp.concatenate([token_sums.reshape(-1), qkv_total, hidden_total]), row_lane
    )
    while up.step < rows:
        up.advance()
    while both.step < rows:
        both.advance()

    token_sums = sums[: 6 * span].reshape(6, span)
    qkv_sums = sums[6 * span : 9 * span]
    hidden_sums = sums[9 * span :]
    qkv = both.result
    return (
        output,
        grad_tokens,
        qkv[:, :span],
        qkv_sums[:span],
        qkv[:, span : 2 * span],
        qkv[:, 2 * span :],
        qkv_sums[2 * span :],
        out.result,
        token_sums[0],
        token_sums[1],
        token_sums[2],
        up.result,
        hidden_sums,
        down.result,
        token_sums[3],
        token_sums[4],
        token_sums[5],
    )


def solution(mesh):
    both, col, back = P("row", "col"), P("col"), P("col", "row")
    return jax.shard_map(
        functools.partial(local, mesh),
        mesh=mesh,
        in_specs=(
            both, both, P("row"), both, col, both, both, col, back, col, col, col, both, col, back,
            col, col, col,
        ),
        out_specs=(
            both, both, both, col, both, both, col, back, col, col, col, both, col, back, col, col,
            col,
        ),
        check_vma=False,
    )
```

```python
import functools

import jax
import jax.numpy as jnp
from jax import lax
from jax.experimental import pallas as pl
from jax.experimental.pallas import tpu as pltpu
from jax.sharding import PartitionSpec as P

HEAD_DIM = 128
LAYERS = 2
SEQ_LEN = 1024

EPSILON = 1e-06
MASKED = -1e30
SCALE = HEAD_DIM ** (-0.5)

bf16 = jnp.bfloat16
f32 = jnp.float32


def dot(left, right):
    return lax.dot_general(left, right, (((1,), (0,)), ((), ())), preferred_element_type=f32)


def dot_t(left, right):
    return lax.dot_general(left, right, (((1,), (1,)), ((), ())), preferred_element_type=f32)


def dot_g(left, right):
    return lax.dot_general(left, right, (((0,), (0,)), ((), ())), preferred_element_type=f32)


def after(value, *others):
    others = [item for item in others if item is not None]
    if not others:
        return value
    return lax.optimization_barrier((value, others))[0]


def attend_kernel(qkv_ref, docs_row_ref, docs_col_ref, mixed_ref, log_ref):
    step = 256
    span = mixed_ref.shape[1]
    key_docs = docs_col_ref[...]
    for head in range(span // HEAD_DIM):
        low = head * HEAD_DIM
        keys = qkv_ref[:, span + low : span + low + HEAD_DIM]
        values_t = qkv_ref[:, 2 * span + low : 2 * span + low + HEAD_DIM].T
        for start in range(0, SEQ_LEN, step):
            query = qkv_ref[start : start + step, low : low + HEAD_DIM]
            scores = dot_t(keys, query) * SCALE
            allowed = key_docs == docs_row_ref[:, start : start + step]
            scores = jnp.where(allowed, scores, MASKED)
            peak = jnp.max(scores, axis=0, keepdims=True)
            weight = jnp.exp(scores - peak)
            total = jnp.sum(weight, axis=0, keepdims=True)
            mixed_t = dot(values_t, weight.astype(bf16)) * (1.0 / total)
            mixed_ref[start : start + step, low : low + HEAD_DIM] = mixed_t.T.astype(bf16)
            log_ref[head, :, start : start + step] = peak + jnp.log(total)


def attend(qkv, span, docs_row, docs_col):
    groups = qkv.shape[1] // (3 * span)
    heads = span // HEAD_DIM
    return pl.pallas_call(
        attend_kernel,
        grid=(groups,),
        in_specs=[
            pl.BlockSpec((SEQ_LEN, 3 * span), lambda g: (0, g)),
            pl.BlockSpec((1, SEQ_LEN), lambda g: (0, 0)),
            pl.BlockSpec((SEQ_LEN, 1), lambda g: (0, 0)),
        ],
        out_specs=[
            pl.BlockSpec((SEQ_LEN, span), lambda g: (0, g)),
            pl.BlockSpec((heads, 1, SEQ_LEN), lambda g: (g, 0, 0)),
        ],
        out_shape=[
            jax.ShapeDtypeStruct((SEQ_LEN, span * groups), bf16),
            jax.ShapeDtypeStruct((heads * groups, 1, SEQ_LEN), f32),
        ],
        compiler_params=pltpu.CompilerParams(vmem_limit_bytes=48 * 1024 * 1024),
        cost_estimate=pl.CostEstimate(
            flops=groups * heads * 8 * SEQ_LEN * SEQ_LEN * HEAD_DIM,
            bytes_accessed=groups * SEQ_LEN * span * 8,
            transcendentals=groups * heads * SEQ_LEN * SEQ_LEN,
        ),
        name="attend",
    )(qkv, docs_row, docs_col)


def attend_back_kernel(
    qkv_ref, grad_ref, log_ref, docs_row_ref, docs_col_ref, out_ref, probs_ref, dscores_ref
):
    step = 256
    span = grad_ref.shape[1]
    key_docs = docs_col_ref[...]
    for head in range(span // HEAD_DIM):
        low = head * HEAD_DIM
        own = slice(low, low + HEAD_DIM)
        keys = qkv_ref[:, span + low : span + low + HEAD_DIM]
        values = qkv_ref[:, 2 * span + low : 2 * span + low + HEAD_DIM]
        for start in range(0, SEQ_LEN, step):
            at = slice(start, start + step)
            scores = dot_t(keys, qkv_ref[at, own]) * SCALE
            allowed = key_docs == docs_row_ref[:, at]
            probs = jnp.exp(jnp.where(allowed, scores, MASKED) - log_ref[head, :, at])
            dprobs = dot_t(values, grad_ref[at, own])
            along = jnp.sum(dprobs * probs, axis=0, keepdims=True)
            probs_ref[:, at] = probs.astype(bf16)
            dscores_ref[:, at] = (probs * (dprobs - along)).astype(bf16)
        dscores = dscores_ref[...]
        out_ref[:, own] = (dot(keys.T, dscores) * SCALE).T.astype(bf16)
        out_ref[:, span + low : span + low + HEAD_DIM] = (
            dot(dscores, qkv_ref[:, own]) * SCALE
        ).astype(bf16)
        out_ref[:, 2 * span + low : 2 * span + low + HEAD_DIM] = dot(
            probs_ref[...], grad_ref[:, own]
        ).astype(bf16)


def attend_back(qkv, grad, log_total, span, docs_row, docs_col):
    groups = qkv.shape[1] // (3 * span)
    heads = span // HEAD_DIM
    return pl.pallas_call(
        attend_back_kernel,
        grid=(groups,),
        in_specs=[
            pl.BlockSpec((SEQ_LEN, 3 * span), lambda g: (0, g)),
            pl.BlockSpec((SEQ_LEN, span), lambda g: (0, g)),
            pl.BlockSpec((heads, 1, SEQ_LEN), lambda g: (g, 0, 0)),
            pl.BlockSpec((1, SEQ_LEN), lambda g: (0, 0)),
            pl.BlockSpec((SEQ_LEN, 1), lambda g: (0, 0)),
        ],
        out_specs=pl.BlockSpec((SEQ_LEN, 3 * span), lambda g: (0, g)),
        out_shape=jax.ShapeDtypeStruct((SEQ_LEN, 3 * span * groups), bf16),
        scratch_shapes=[pltpu.VMEM((SEQ_LEN, SEQ_LEN), bf16)] * 2,
        compiler_params=pltpu.CompilerParams(vmem_limit_bytes=48 * 1024 * 1024),
        cost_estimate=pl.CostEstimate(
            flops=groups * heads * 20 * SEQ_LEN * SEQ_LEN * HEAD_DIM,
            bytes_accessed=groups * SEQ_LEN * span * 16,
            transcendentals=groups * heads * SEQ_LEN * SEQ_LEN,
        ),
        name="attend_back",
    )(qkv, grad, log_total, docs_row, docs_col)


class Place:
    def __init__(self, mesh, own_rows):
        self.own_rows = own_rows
        self.rows = mesh.shape["row"]
        self.cols = mesh.shape["col"]
        self.a = self.cols // 2
        self.b = self.cols // 4
        self.rest = []
        mask = 1
        while mask < self.b:
            self.rest.append(mask)
            mask *= 2
        self.row = lax.axis_index("row")
        self.col = lax.axis_index("col")
        order = [0]
        for mask in self.rest:
            order = order + [item ^ mask for item in order]
        self.order = order

    def bit(self, mask):
        return (self.col // mask) % 2

    def swap(self, value, mask):
        return lax.ppermute(value, "col", [(i, i ^ mask) for i in range(self.cols)])

    def shift(self, value):
        return lax.ppermute(value, "row", [(i, (i + 1) % self.rows) for i in range(self.rows)])

    def on(self, lane, value, mask):
        if lane is None:
            return self.swap(value, mask)
        return lane.send(lambda item: self.swap(item, mask), value)

    def tokens_send(self, value, mask, lane, inner=1):
        width = value.shape[-1]
        split = value.reshape(-1, 2, inner * self.own_rows, width)
        bit = self.bit(mask)
        mine = lax.dynamic_index_in_dim(split, bit, 1, keepdims=False).reshape(-1, width)
        sent = lax.dynamic_index_in_dim(split, 1 - bit, 1, keepdims=False).reshape(-1, width)
        return (mine, self.on(lane, sent, mask))

    def tokens_merge(self, mine, got, mask, groups=1):
        part = mine.shape[-1] // groups
        return jnp.concatenate(
            [
                self.ordered(
                    mine[:, i * part : (i + 1) * part], got[:, i * part : (i + 1) * part], mask, 1
                )
                for i in range(groups)
            ],
            axis=1,
        )

    def features_send(self, value, mask, lane, groups=1):
        width = value.shape[2] // (2 * groups)
        bit = self.bit(mask)

        def pick(side):
            return jnp.concatenate(
                [
                    lax.dynamic_slice_in_dim(value, (2 * i + side) * width, width, 2)
                    for i in range(groups)
                ],
                axis=2,
            )

        return (pick(bit), self.on(lane, pick(1 - bit), mask))

    def features_merge(self, mine, got, mask, axis):
        value = self.ordered(jnp.expand_dims(mine, axis), jnp.expand_dims(got, axis), mask, axis)
        return value.reshape(-1, *mine.shape[1:])

    def ordered(self, mine, got, mask, axis):
        low = self.bit(mask) == 0
        return jnp.concatenate(
            [jnp.where(low, mine, got), jnp.where(low, got, mine)], axis=axis
        )

    def all_features(self, value, lane_of):
        for mask in self.rest + [self.b, self.a]:
            value = self.ordered(value, self.on(lane_of(mask), value, mask), mask, 1)
        return value


    def blocks(self, value, pieces, axis):
        size = pieces[0].shape[axis] // self.rows
        found = []
        for step in range(self.rows):
            at = ((self.row - 1 - step + 2 * self.rows) % self.rows) * size
            found.append(
                jnp.concatenate(
                    [lax.dynamic_slice_in_dim(item, at, size, axis) for item in pieces], axis=value
                )
            )
        return found

    def parts(self, sums, mask):
        width = sums.shape[1] // 2
        bit = self.bit(mask)
        return (
            lax.dynamic_slice_in_dim(sums, bit * width, width, 1),
            lax.dynamic_slice_in_dim(sums, (1 - bit) * width, width, 1),
        )

    def halve(self, sums, mask, lane):
        mine, sent = self.parts(sums, mask)
        return mine + self.on(lane, sent, mask)

    def row_sum(self, value):
        mask = 1
        while mask < self.rows:
            pairs = [(i, i ^ mask) for i in range(self.rows)]
            value = value + lax.ppermute(value, "row", pairs)
            mask *= 2
        return value


def norm_forward(residual, gain, shift):
    mean = jnp.mean(residual, axis=1, keepdims=True)
    center = residual - mean
    inverse = lax.rsqrt(jnp.mean(center * center, axis=1, keepdims=True) + EPSILON)
    normed = center * inverse
    return (normed * gain + shift, normed, inverse)


def norm_backward(grad, normed, inverse, gain):
    scaled = grad * gain
    mean = jnp.mean(scaled, axis=1, keepdims=True)
    along = jnp.mean(scaled * normed, axis=1, keepdims=True)
    result = inverse * (scaled - mean - normed * along)
    return (result, jnp.sum(grad * normed, axis=0), jnp.sum(grad, axis=0))


def gelu(value):
    return jax.nn.gelu(value, approximate=True)


def gelu_slope(value):
    inner = 0.7978845608028654
    cubic = 0.044715
    square = value * value
    tangent = jnp.tanh(inner * value * (1.0 + cubic * square))
    return 0.5 * (1.0 + tangent) + 0.5 * value * (1.0 - tangent * tangent) * inner * (
        1.0 + 3.0 * cubic * square
    )


class Clock:
    def __init__(self):
        self.last = None

    def hold(self, value, *others):
        return after(value, self.last, *others)

    def run(self, work, *args):
        self.last = work(*self.hold(args))
        return self.last

    def wait(self, *results):
        self.last = (self.last, results)

    def aside(self, work, *args):
        return work(*self.hold(args))


class Lane:
    def __init__(self, clock, width=1):
        self.clock = clock
        self.width = width
        self.done = []

    def send(self, move, value):
        wait = self.done[-self.width] if len(self.done) >= self.width else None
        result = move(after(value, wait))
        self.done.append(result)
        return result


class Weights:
    def __init__(self, place, clock, ring, blocks):
        self.place, self.clock, self.ring = place, clock, ring
        self.entries = blocks
        self.own = {name: [entry[1]] for name, entry in blocks.items()}
        self.other = {name: [] for name in blocks}
        self.wholes = {}

    def exchange(self, name):
        whole, block, far, lane, axis, corner, spans = self.entries[name]
        step = len(self.other[name])
        self.other[name].append(
            lane.send(lambda value: self.place.swap(value, far), self.own[name][step])
        )

    def exchange_all(self, name):
        whole, block, far, lane, axis, corner, spans = self.entries[name]
        blocks = jnp.concatenate(self.own[name], axis=0)
        got = lane.send(lambda value: self.place.swap(value, far), blocks)
        self.other[name] = jnp.split(got, self.place.rows, axis=0)

    def step(self, name):
        self.own[name].append(self.ring.send(self.place.shift, self.own[name][-1]))

    def arrived(self, step, *names):
        self.clock.wait([self.own[name][step] for name in names])

    def put(self, name, step, side):
        place = self.place
        whole, block, far, lane, axis, corner, spans = self.entries[name]
        items = self.other if side else self.own
        at = ((place.row - step + place.rows) % place.rows) * spans[axis] + corner[axis]
        start = [0, 0]
        start[axis] = at
        start[1 - axis] = side * spans[1 - axis] + corner[1 - axis]
        if whole not in self.wholes:
            shape = [0, 0]
            shape[axis], shape[1 - axis] = place.rows * spans[axis], 2 * spans[1 - axis]
            self.wholes[whole] = jnp.full(shape, len(self.wholes), block.dtype)
        self.wholes[whole] = self.clock.run(
            lambda total, item: lax.dynamic_update_slice(total, item, start),
            self.wholes[whole],
            items[name][step],
        )


def entry(name, block, far, lane, axis):
    return {name: (name, block, far, lane, axis, (0, 0), block.shape)}


def halves(name, block, far, lane, axis):
    half = block.shape[0] // 2
    return {
        name + "0": (name, block[:half], far, lane, axis, (0, 0), block.shape),
        name + "1": (name, block[half:], far, lane, axis, (half, 0), block.shape),
    }


def join(pair):
    return jnp.concatenate(pair, axis=0)


def columns(pair, split):
    return (join([item[:, :split] for item in pair]), join([item[:, split:] for item in pair]))


class Exchange:
    def __init__(self, place, clock, lane, far):
        self.place, self.clock, self.lane, self.bit = place, clock, lane, far

    def far(self, value):
        return self.lane.send(lambda item: self.place.swap(item, self.bit), value)

    def near(self, value):
        for mask in self.place.rest:
            value = self.clock.run(
                lambda own, got: jnp.concatenate([own, got], axis=0),
                value,
                self.place.swap(self.clock.hold(value), mask),
            )
        return value

    def halved(self, terms):
        for mask in self.place.rest[::-1]:
            half = terms.shape[0] // 2
            got = self.place.swap(self.clock.hold(terms[half:]), mask)
            if mask == self.place.rest[0]:
                return (terms[:half], got)
            terms = self.clock.run(
                lambda own, more: (own.astype(f32) + more.astype(f32)).astype(bf16),
                terms[:half],
                got,
            )
        return (terms, jnp.zeros_like(terms))

    def sum_far(self, terms, meanwhile=None):
        kept, got = self.halved(terms)
        if meanwhile is not None:
            meanwhile()
        part = self.clock.run(
            lambda own, more: (own.astype(f32) + more.astype(f32)).astype(bf16), kept, got
        )
        return self.far(part)


def plus(*items):
    total = items[0].astype(f32)
    for item in items[1:]:
        total = total + item.astype(f32)
    return total


def local(
    mesh,
    tokens,
    cotangent,
    segments,
    query_weight,
    query_bias,
    key_weight,
    value_weight,
    value_bias,
    output_weight,
    output_bias,
    first_gain,
    first_shift,
    up_weight,
    up_bias,
    down_weight,
    down_bias,
    second_gain,
    second_shift,
):
    place = Place(mesh, tokens.shape[0] // mesh.shape["col"])
    clock = Clock()
    run = clock.run
    rows = place.rows
    steps = range(1, rows)
    span = query_weight.shape[1]
    hidden_span = up_weight.shape[1]
    own_rows = place.own_rows
    lane_a, lane_b, row_lane = Lane(clock), Lane(clock), Lane(clock)
    across_b = Exchange(place, clock, lane_b, place.b)
    across_a = Exchange(place, clock, lane_a, place.a)

    def on_lane(mask):
        return lane_a if mask == place.a else lane_b if mask == place.b else None

    def project(rows_in, weight, bias):
        return (dot(rows_in, weight) + bias).astype(bf16)

    def up_product(rows_in, weight, bias):
        hidden = dot(rows_in, weight) + bias
        return (hidden, gelu(hidden).astype(bf16))

    def product(rows_in, weight):
        return dot(rows_in, weight).astype(bf16)

    def norm(residual, kept, got, sent, bias, gain, shift):
        result, normed, inverse = norm_forward(plus(residual, kept, got, sent) + bias, gain, shift)
        return (result, result.astype(bf16), normed, inverse)

    w_all = jnp.concatenate([query_weight, key_weight, value_weight], axis=1)
    ring = Weights(
        place,
        clock,
        row_lane,
        {
            **entry("qkv", w_all, place.a, lane_a, 0),
            **entry("out", output_weight, place.a, lane_a, 1),
            **entry("up", up_weight, place.b, lane_b, 0),
            **halves("down", down_weight, place.b, lane_b, 1),
        },
    )

    def steps_of(*names):
        for name in names:
            ring.step(name)

    def exchanges(*names):
        for name in names:
            ring.exchange(name)

    def puts(step, side, *names):
        for name in names:
            ring.put(name, step, side)

    def merge(mask, groups=1):
        return lambda mine, got: place.tokens_merge(mine, got, mask, groups)

    def blocks(*pieces):
        return place.blocks(0, pieces, 1)

    exchanges("qkv")
    steps_of("qkv")
    value = tokens
    for mask in place.rest:
        value = run(merge(mask), *place.tokens_send(value, mask, None))
    value = place.tokens_send(value, place.b, lane_b)
    vectors = jnp.stack(
        [output_bias, first_gain, first_shift, down_bias, second_gain, second_shift]
    )
    for mask in place.rest:
        vectors = place.ordered(vectors, place.swap(vectors, mask), mask, 1)
    got, up_bias_other = lane_b.send(
        lambda items: tuple(place.swap(item, place.b) for item in items), (vectors, up_bias)
    )
    vectors = place.ordered(vectors, got, place.b, 1)
    b_up = jnp.concatenate([up_bias, up_bias_other])
    exchanges("up")
    puts(0, 0, "qkv", "out")
    masks = place.order + [item ^ place.b for item in place.order]
    docs = jnp.concatenate(
        [
            lax.dynamic_slice_in_dim(
                segments, jnp.bitwise_xor(place.col, mask) * own_rows, own_rows, 0
            )
            for mask in masks
        ]
    )
    docs = (docs[None, :], docs[:, None])
    value = run(merge(place.b), *value)
    value = place.tokens_send(value, place.a, lane_a)
    ring.arrived(1, "qkv")
    steps_of("qkv")
    puts(0, 1, "qkv")
    pair = jnp.concatenate([query_bias, jnp.zeros_like(query_bias), value_bias])
    pair_other, got = lane_a.send(
        lambda items: tuple(place.swap(item, place.a) for item in items), (pair, vectors)
    )
    b_qkv = jnp.concatenate([pair, pair_other])
    vectors = place.ordered(vectors, got, place.a, 1)
    b_out, gain1, shift1, b_down, gain2, shift2 = (vectors[i] for i in range(6))
    puts(1, 0, "qkv")
    for step in range(1, rows):
        exchanges("qkv")
        if step < rows - 2:
            steps_of("qkv")
    state_low = run(merge(place.a), *value)
    state = state_low.astype(f32)
    far = across_b.far(state_low)
    exchanges("down0", "down1")
    own = across_b.near(state_low)
    clock.wait(b_qkv, b_up, vectors)
    for step in range(2, rows):
        ring.arrived(step, "qkv")
        if step == rows - 1:
            steps_of("out")
        puts(step, 0, "qkv")
        puts(step - 1, 1, "qkv")
    for step in range(1, rows):
        ring.arrived(step, "out")
        steps_of("out" if step < rows - 1 else "up")
        puts(step, 0, "out")
    ring.exchange_all("out")
    other = across_b.near(far)
    puts(0, 0, "up")
    puts(0, 1, "up")
    puts(rows - 1, 1, "qkv")
    w_qkv = ring.wholes["qkv"]
    clock.wait(ring.other["down0"][0])
    qkv_own = run(project, own, w_qkv, b_qkv)
    ring.arrived(1, "up")
    steps_of("up")
    clock.wait(ring.other["down1"][0])
    exchanges("up")
    qkv_other = run(project, other, w_qkv, b_qkv)
    qkv = run(lambda *items: join(items), qkv_own, qkv_other)
    puts(1, 0, "up")
    ring.arrived(2, "up")
    steps_of("up" if rows > 3 else "down0")
    mixed, log_total = run(lambda item: attend(item, span, *docs), qkv)
    clock.wait(ring.other["up"][1])
    for step in range(rows):
        puts(step, 1, "out")
    w_out = ring.wholes["out"]
    half = mixed.shape[0] // 2
    terms_other = run(product, mixed[half:], w_out)
    terms_own = []

    def meanwhile():
        terms_own.append(run(product, mixed[:half], w_out))
        puts(1, 1, "up")

    sent = across_b.sum_far(terms_other, meanwhile)
    sums = across_b.halved(terms_own[0])
    exchanges("up")
    puts(2, 0, "up")
    for step in range(3, rows):
        ring.arrived(step, "up")
        steps_of("up" if step < rows - 1 else "down0")
        exchanges("up")
        puts(step, 0, "up")
    puts(0, 0, "down0", "down1")
    puts(0, 1, "down0", "down1")
    far_half = ring.entries["down1"]
    corner = (far_half[5][0] + far_half[6][0], 0)
    ring.entries["more"] = (*far_half[:5], corner, far_half[6])
    ring.own["more"] = ring.other["down1"]
    queue = ["down0"] * (rows - 2) + ["down1", "more"] * (rows - 1)
    first, first_low, normed1, inverse1 = run(norm, state, *sums, sent, b_out, gain1, shift1)
    far = across_a.far(first_low)
    ring.arrived(1, "down0")
    steps_of(queue.pop(0))
    exchanges("down0")
    own_first = across_a.near(first_low)
    puts(2, 1, "up")
    puts(1, 0, "down0")
    ring.arrived(2, "down0")
    steps_of(queue.pop(0))
    exchanges("down0")
    puts(2, 0, "down0")
    other_first = across_a.near(far)
    for step in range(3, rows):
        ring.arrived(step, "down0")
        steps_of(queue.pop(0))
        exchanges("down0")
        puts(step, 1, "up")
        puts(step, 0, "down0")
    w_up = ring.wholes["up"]
    ring.arrived(1, "down1")
    steps_of(queue.pop(0))
    hidden_own, active_own = run(up_product, own_first, w_up, b_up)
    ring.arrived(1, "more")
    steps_of(queue.pop(0))
    hidden_other, active_other = run(up_product, other_first, w_up, b_up)
    ring.arrived(2, "down1")
    steps_of(queue.pop(0))
    puts(1, 1, "down0")
    puts(1, 0, "down1", "more")
    token_pieces = run(blocks, own, other)
    ring.arrived(2, "more")
    if queue:
        steps_of(queue.pop(0))
    puts(2, 1, "down0")
    puts(2, 0, "down1", "more")
    first_pieces = run(blocks, own_first, other_first)
    for step in range(3, rows):
        ring.arrived(step, "down1")
        if queue:
            steps_of(queue.pop(0))
        puts(step, 1, "down0")
        puts(step, 0, "down1")
        if step == 3:
            active_sides = run(
                lambda *items: columns(items, hidden_span), active_own, active_other
            )
        ring.arrived(step, "more")
        if queue:
            steps_of(queue.pop(0))
        if step < rows - 1:
            puts(step, 0, "more")
    if rows > 3:
        puts(rows - 1, 0, "more")
    w_down = ring.wholes["down"]
    terms_other = run(product, active_other, w_down)
    sent = across_a.sum_far(terms_other)
    terms_own = run(product, active_own, w_down)
    sums = across_a.halved(terms_own)
    kept_attention = [(token_pieces, qkv, mixed, log_total, normed1, inverse1)]
    state, state_low, normed2, inverse2 = run(
        norm, first, *sums, sent, b_down, gain2, shift2
    )
    kept_feed = [(first_pieces, (hidden_own, hidden_other), active_sides, normed2, inverse2)]

    grad = cotangent
    for mask in place.rest:
        grad = clock.aside(merge(mask), *place.tokens_send(grad, mask, None))
    for depth in range(1, LAYERS):
        far = across_b.far(state_low)
        own = across_b.near(state_low)
        qkv_own = run(project, own, w_qkv, b_qkv)
        other = across_b.near(far)
        qkv_other = run(project, other, w_qkv, b_qkv)
        qkv = run(lambda *items: join(items), qkv_own, qkv_other)
        if depth == 1:
            grad = place.tokens_send(grad, place.a, lane_a, 2)
        mixed, log_total = run(lambda item: attend(item, span, *docs), qkv)
        if depth == 1:
            clock.wait(grad[1])
        terms_other = run(product, mixed[half:], w_out)
        terms_own = []
        sent = across_b.sum_far(
            terms_other, lambda: terms_own.append(run(product, mixed[:half], w_out))
        )
        sums = across_b.halved(terms_own[0])
        token_pieces = run(blocks, own, other)
        if depth == 1:
            grad = run(merge(place.a), *grad)
        first, first_low, normed1, inverse1 = run(norm, state, *sums, sent, b_out, gain1, shift1)
        kept_attention.append((token_pieces, qkv, mixed, log_total, normed1, inverse1))
        far = across_a.far(first_low)
        own = across_a.near(first_low)
        if depth == 1:
            grad = place.tokens_send(grad, place.b, lane_b)
        hidden_own, active_own = run(up_product, own, w_up, b_up)
        terms_own = run(product, active_own, w_down)
        own_sums = across_a.halved(terms_own)
        if depth == 1:
            clock.wait(grad[1])
        other = across_a.near(far)
        hidden_other, active_other = run(up_product, other, w_up, b_up)
        terms_other = run(product, active_other, w_down)
        sent = across_a.sum_far(terms_other)
        if depth == 1:
            grad = run(merge(place.b, 2), *grad)
        first_pieces = run(blocks, own, other)
        active_sides = run(lambda *items: columns(items, hidden_span), active_own, active_other)
        state, state_low, normed2, inverse2 = run(
            norm, first, *own_sums, sent, b_down, gain2, shift2
        )
        kept_feed.append(
            (first_pieces, (hidden_own, hidden_other), active_sides, normed2, inverse2)
        )
    output = state_low[None]

    def gelu_back(rows_in, weight, hidden):
        return (dot_t(rows_in, weight) * gelu_slope(hidden)).astype(bf16)

    def product_t(rows_in, weight):
        return dot_t(rows_in, weight).astype(bf16)

    def norm_back(grads, normed, inverse, gain):
        result, gain_grad, shift_grad = norm_backward(plus(*grads), normed, inverse, gain)
        low = result.astype(bf16)
        return (result, low, jnp.stack([jnp.sum(low, axis=0, dtype=f32), gain_grad, shift_grad]))

    def sum_rows(*items):
        return jnp.concatenate([jnp.sum(item, axis=0, dtype=f32) for item in items])

    class Share:
        def __init__(self, name, left, right, lane, far):
            self.name, self.left, self.right = name, left, right
            self.lane, self.far = lane, far
            self.before = held.get(name)
            self.got = []
            self.sent = []
            self.total = None
            self.step = 0

        def keep(self):
            left, right = clock.hold((self.left, self.right))
            clock.last = [
                [dot_g(left[side][step], right[side][step]) for step in range(rows)]
                for side in (0, 1)
            ]
            held[self.name] = clock.last

        def other_first(self):
            self.other(1)

        def other(self, count=None):
            for step in range(len(self.sent), rows if count is None else count):
                left, right = clock.hold((self.left[1][step], self.right[1][step]))
                clock.last = (dot_g(left, right) + self.before[1][step]).astype(bf16)
                self.sent.append(clock.last)

        def send(self, count=1):
            for step in range(count):
                self.got.append(
                    self.lane.send(
                        lambda item: place.swap(item, self.far), self.sent[len(self.got)]
                    )
                )

        def send_all(self):
            got = self.lane.send(
                lambda item: place.swap(item, self.far), jnp.concatenate(self.sent, axis=0)
            )
            self.got = jnp.split(got, rows, axis=0)

        def advance(self):
            step = self.step
            more = [self.got[step]] + ([] if self.total is None else [self.total])
            left, right, before, more = clock.hold(
                (self.left[0][step], self.right[0][step], self.before[0][step], more)
            )
            value = dot_g(left, right) + before
            for item in more:
                value = value + item.astype(f32)
            self.step += 1
            if step < rows - 1:
                value = value.astype(bf16)
            clock.last = self.result = value
            if step < rows - 1:
                self.total = row_lane.send(place.shift, value)

    held = {}
    norm_sums, qkv_sums, hidden_sums = [], [], []
    grads = (grad,)
    for depth in reversed(range(LAYERS)):
        last = depth == 0
        token_pieces, qkv, mixed, log_total, normed1, inverse1 = kept_attention[depth]
        first_pieces, hiddens, (active_own, active_other), normed2, inverse2 = kept_feed[depth]
        dr2, dsecond, sums2 = run(norm_back, grads, normed2, inverse2, gain2)
        far = across_a.far(dsecond)
        second_own = across_a.near(dsecond)
        if not last:
            output = place.features_send(output, place.b, lane_b, 2)
        dhid_own = run(gelu_back, second_own, w_down, hiddens[0])
        terms_own = run(product_t, dhid_own, w_up)
        own_sums = across_a.halved(terms_own)
        second_other = across_a.near(far)

        def down_share():
            pieces = run(blocks, second_own, second_other)
            return Share(
                "down",
                ([active_own] * rows, [active_other] * rows),
                (pieces, pieces),
                lane_b,
                place.b,
            )

        if last:
            down = down_share()
            down.other()
            down.send(3)
        dhid_other = run(gelu_back, second_other, w_down, hiddens[1])
        terms_other = run(product_t, dhid_other, w_up)
        if not last:
            clock.wait(output[1])
            output = clock.aside(lambda *items: place.features_merge(*items, place.b, 1), *output)
        sides = []
        sent = across_a.sum_far(
            terms_other,
            lambda: sides.extend(
                run(lambda *items: columns(items, hidden_span), dhid_own, dhid_other)
            ),
        )
        dhid_left, dhid_right = sides
        if last:
            down.advance()
        up = Share(
            "up",
            (first_pieces, first_pieces),
            ([dhid_left] * rows, [dhid_right] * rows),
            lane_b,
            place.b,
        )
        if last:
            up.other()
            hidden_total = hidden_sums[0] + clock.aside(sum_rows, dhid_left, dhid_right)
        else:
            down = down_share()
            down.keep()
        dr1, dbranch, sums1 = run(norm_back, (dr2, *own_sums, sent), normed1, inverse1, gain1)
        norm_sums.append(jnp.concatenate([sums1, sums2], axis=0))
        far = across_b.far(dbranch)
        branch_own = across_b.near(dbranch)
        dmixed_own = run(product_t, branch_own, w_out)
        if last:
            token_sums = place.halve(sum(norm_sums), place.a, lane_a)
            down.advance()
            down.send(rows - 3)
            up.send()
        else:
            output = place.features_send(output, place.a, lane_a)
            up.keep()
            clock.wait(output[1])
            hidden_sums.append(clock.aside(sum_rows, dhid_left, dhid_right))
        branch_other = across_b.near(far)
        dmixed_other = run(product_t, branch_other, w_out)
        dmixed = run(lambda *items: join(items), dmixed_own, dmixed_other)
        pieces = run(blocks, branch_own, branch_other)
        out = Share(
            "out",
            ([mixed[:, :span]] * rows, [mixed[:, span:]] * rows),
            (pieces, pieces),
            lane_a,
            place.a,
        )
        if last:
            out.other()
            out.send_all()
            down.advance()
            clock.wait(up.got[0])
            up.send()
        else:
            output = clock.aside(lambda *items: place.features_merge(*items, place.a, 0), *output)
        dqkv = run(lambda *items: attend_back(*items, log_total, span, *docs), qkv, dmixed)
        qkv_sums.append(clock.aside(sum_rows, dqkv))
        if last:
            clock.wait(out.got, up.got[1])
            while down.step < rows:
                down.advance()
            up.advance()
        terms_other = run(product_t, dqkv[half:], w_qkv)
        if last:
            both = Share(
                "qkv",
                (token_pieces, token_pieces),
                ([dqkv[:, : 3 * span]] * rows, [dqkv[:, 3 * span :]] * rows),
                lane_a,
                place.a,
            )
            sent = across_b.sum_far(terms_other, both.other_first)
            both.send()
        else:
            terms_own = []
            sent = across_b.sum_far(
                terms_other, lambda: terms_own.append(run(product_t, dqkv[:half], w_qkv))
            )
            own_sums = across_b.halved(terms_own[0])
        if not last:
            both = Share(
                "qkv",
                (token_pieces, token_pieces),
                ([dqkv[:, : 3 * span]] * rows, [dqkv[:, 3 * span :]] * rows),
                lane_a,
                place.a,
            )
        if last:
            both.other()
            clock.wait(both.got[0], sent)
            both.send()
            up.send()
            up.advance()
        if last:
            terms_own = run(product_t, dqkv[:half], w_qkv)
            own_sums = across_b.halved(terms_own)
        else:
            out.keep()
            both.keep()
        grads = (dr1, *own_sums, sent)
    clock.wait(own_sums)
    for step in range(rows):
        out.advance()
    grad = run(lambda *items: plus(*items).astype(bf16)[None], *grads)
    grad = place.features_send(grad, place.a, lane_a)
    both.send(rows - 2)
    both.advance()
    grad = run(lambda *items: place.features_merge(*items, place.a, 0), *grad)
    up.send(rows - len(up.got))
    grad = place.features_send(grad, place.b, lane_b)
    up.advance()
    both.advance()
    grad = run(lambda *items: place.features_merge(*items, place.b, 1), *grad)
    for mask in place.rest[::-1]:
        grad = run(
            lambda *items: place.features_merge(*items, mask, 1),
            *place.features_send(grad, mask, None),
        )
    grad_tokens = grad.reshape(-1, span).astype(f32)
    for mask in place.rest[::-1]:
        output = run(
            lambda *items: place.features_merge(*items, mask, 1),
            *place.features_send(output, mask, None),
        )
    output = output.reshape(-1, span)
    qkv_total = sum(qkv_sums)
    qkv_total = qkv_total[: 3 * span] + lane_a.send(
        lambda item: place.swap(item, place.a), qkv_total[3 * span :]
    )
    mine, away = place.parts(token_sums, place.b)
    more = lane_b.send(
        lambda items: tuple(place.swap(item, place.b) for item in items),
        (away, hidden_total[hidden_span:]),
    )
    token_sums = mine + more[0]
    hidden_total = hidden_total[:hidden_span] + more[1]
    for mask in place.rest[::-1]:
        token_sums = place.halve(token_sums, mask, None)
    while both.step < rows - 1:
        both.advance()
        if up.step < rows:
            up.advance()
    sums = place.row_sum(
        jnp.concatenate([token_sums.reshape(-1), qkv_total, hidden_total])
    )
    while up.step < rows:
        up.advance()
    while both.step < rows:
        both.advance()

    token_sums = sums[: 6 * span].reshape(6, span)
    qkv_sums = sums[6 * span : 9 * span]
    hidden_sums = sums[9 * span :]
    qkv = both.result
    return (
        output,
        grad_tokens,
        qkv[:, :span],
        qkv_sums[:span],
        qkv[:, span : 2 * span],
        qkv[:, 2 * span :],
        qkv_sums[2 * span :],
        out.result,
        token_sums[0],
        token_sums[1],
        token_sums[2],
        up.result,
        hidden_sums,
        down.result,
        token_sums[3],
        token_sums[4],
        token_sums[5],
    )


def solution(mesh):
    both, col, back = P("row", "col"), P("col"), P("col", "row")
    return jax.shard_map(
        functools.partial(local, mesh),
        mesh=mesh,
        in_specs=(
            both, both, P("row"), both, col, both, both, col, back, col, col, col, both, col, back,
            col, col, col,
        ),
        out_specs=(
            both, both, both, col, both, both, col, back, col, col, col, both, col, back, col, col,
            col,
        ),
        check_vma=False,
    )
```

```python
import functools

import jax
import jax.numpy as jnp
from jax import lax
from jax.experimental import pallas as pl
from jax.experimental.pallas import tpu as pltpu
from jax.sharding import PartitionSpec as P

HEAD_DIM = 128
LAYERS = 2
SEQ_LEN = 1024

EPSILON = 1e-06
MASKED = -1e30
SCALE = HEAD_DIM ** (-0.5)

bf16 = jnp.bfloat16
f32 = jnp.float32


def dot(left, right):
    return lax.dot_general(left, right, (((1,), (0,)), ((), ())), preferred_element_type=f32)


def dot_t(left, right):
    return lax.dot_general(left, right, (((1,), (1,)), ((), ())), preferred_element_type=f32)


def dot_g(left, right):
    return lax.dot_general(left, right, (((0,), (0,)), ((), ())), preferred_element_type=f32)


def after(value, *others):
    others = [item for item in others if item is not None]
    if not others:
        return value
    return lax.optimization_barrier((value, others))[0]


def attend_kernel(qkv_ref, docs_row_ref, docs_col_ref, mixed_ref, log_ref):
    step = 256
    span = mixed_ref.shape[1]
    key_docs = docs_col_ref[...]
    for head in range(span // HEAD_DIM):
        low = head * HEAD_DIM
        keys = qkv_ref[:, span + low : span + low + HEAD_DIM]
        values_t = qkv_ref[:, 2 * span + low : 2 * span + low + HEAD_DIM].T
        for start in range(0, SEQ_LEN, step):
            query = qkv_ref[start : start + step, low : low + HEAD_DIM]
            scores = dot_t(keys, query) * SCALE
            allowed = key_docs == docs_row_ref[:, start : start + step]
            scores = jnp.where(allowed, scores, MASKED)
            peak = jnp.max(scores, axis=0, keepdims=True)
            weight = jnp.exp(scores - peak)
            total = jnp.sum(weight, axis=0, keepdims=True)
            mixed_t = dot(values_t, weight.astype(bf16)) * (1.0 / total)
            mixed_ref[start : start + step, low : low + HEAD_DIM] = mixed_t.T.astype(bf16)
            log_ref[head, :, start : start + step] = peak + jnp.log(total)


def attend(qkv, span, docs_row, docs_col):
    groups = qkv.shape[1] // (3 * span)
    heads = span // HEAD_DIM
    return pl.pallas_call(
        attend_kernel,
        grid=(groups,),
        in_specs=[
            pl.BlockSpec((SEQ_LEN, 3 * span), lambda g: (0, g)),
            pl.BlockSpec((1, SEQ_LEN), lambda g: (0, 0)),
            pl.BlockSpec((SEQ_LEN, 1), lambda g: (0, 0)),
        ],
        out_specs=[
            pl.BlockSpec((SEQ_LEN, span), lambda g: (0, g)),
            pl.BlockSpec((heads, 1, SEQ_LEN), lambda g: (g, 0, 0)),
        ],
        out_shape=[
            jax.ShapeDtypeStruct((SEQ_LEN, span * groups), bf16),
            jax.ShapeDtypeStruct((heads * groups, 1, SEQ_LEN), f32),
        ],
        compiler_params=pltpu.CompilerParams(vmem_limit_bytes=48 * 1024 * 1024),
        cost_estimate=pl.CostEstimate(
            flops=groups * heads * 8 * SEQ_LEN * SEQ_LEN * HEAD_DIM,
            bytes_accessed=groups * SEQ_LEN * span * 8,
            transcendentals=groups * heads * SEQ_LEN * SEQ_LEN,
        ),
        name="attend",
    )(qkv, docs_row, docs_col)


def attend_back_kernel(
    qkv_ref, grad_ref, log_ref, docs_row_ref, docs_col_ref, out_ref, probs_ref, dscores_ref
):
    step = 256
    span = grad_ref.shape[1]
    key_docs = docs_col_ref[...]
    for head in range(span // HEAD_DIM):
        low = head * HEAD_DIM
        own = slice(low, low + HEAD_DIM)
        keys = qkv_ref[:, span + low : span + low + HEAD_DIM]
        values = qkv_ref[:, 2 * span + low : 2 * span + low + HEAD_DIM]
        for start in range(0, SEQ_LEN, step):
            at = slice(start, start + step)
            scores = dot_t(keys, qkv_ref[at, own]) * SCALE
            allowed = key_docs == docs_row_ref[:, at]
            probs = jnp.exp(jnp.where(allowed, scores, MASKED) - log_ref[head, :, at])
            dprobs = dot_t(values, grad_ref[at, own])
            along = jnp.sum(dprobs * probs, axis=0, keepdims=True)
            probs_ref[:, at] = probs.astype(bf16)
            dscores_ref[:, at] = (probs * (dprobs - along)).astype(bf16)
        dscores = dscores_ref[...]
        out_ref[:, own] = (dot(keys.T, dscores) * SCALE).T.astype(bf16)
        out_ref[:, span + low : span + low + HEAD_DIM] = (
            dot(dscores, qkv_ref[:, own]) * SCALE
        ).astype(bf16)
        out_ref[:, 2 * span + low : 2 * span + low + HEAD_DIM] = dot(
            probs_ref[...], grad_ref[:, own]
        ).astype(bf16)


def attend_back(qkv, grad, log_total, span, docs_row, docs_col):
    groups = qkv.shape[1] // (3 * span)
    heads = span // HEAD_DIM
    return pl.pallas_call(
        attend_back_kernel,
        grid=(groups,),
        in_specs=[
            pl.BlockSpec((SEQ_LEN, 3 * span), lambda g: (0, g)),
            pl.BlockSpec((SEQ_LEN, span), lambda g: (0, g)),
            pl.BlockSpec((heads, 1, SEQ_LEN), lambda g: (g, 0, 0)),
            pl.BlockSpec((1, SEQ_LEN), lambda g: (0, 0)),
            pl.BlockSpec((SEQ_LEN, 1), lambda g: (0, 0)),
        ],
        out_specs=pl.BlockSpec((SEQ_LEN, 3 * span), lambda g: (0, g)),
        out_shape=jax.ShapeDtypeStruct((SEQ_LEN, 3 * span * groups), bf16),
        scratch_shapes=[pltpu.VMEM((SEQ_LEN, SEQ_LEN), bf16)] * 2,
        compiler_params=pltpu.CompilerParams(vmem_limit_bytes=48 * 1024 * 1024),
        cost_estimate=pl.CostEstimate(
            flops=groups * heads * 20 * SEQ_LEN * SEQ_LEN * HEAD_DIM,
            bytes_accessed=groups * SEQ_LEN * span * 16,
            transcendentals=groups * heads * SEQ_LEN * SEQ_LEN,
        ),
        name="attend_back",
    )(qkv, grad, log_total, docs_row, docs_col)


class Place:
    def __init__(self, mesh, own_rows):
        self.own_rows = own_rows
        self.rows = mesh.shape["row"]
        self.cols = mesh.shape["col"]
        self.a = self.cols // 2
        self.b = self.cols // 4
        self.rest = []
        mask = 1
        while mask < self.b:
            self.rest.append(mask)
            mask *= 2
        self.row = lax.axis_index("row")
        self.col = lax.axis_index("col")
        order = [0]
        for mask in self.rest:
            order = order + [item ^ mask for item in order]
        self.order = order

    def bit(self, mask):
        return (self.col // mask) % 2

    def swap(self, value, mask):
        return lax.ppermute(value, "col", [(i, i ^ mask) for i in range(self.cols)])

    def shift(self, value):
        return lax.ppermute(value, "row", [(i, (i + 1) % self.rows) for i in range(self.rows)])

    def on(self, lane, value, mask):
        if lane is None:
            return self.swap(value, mask)
        return lane.send(lambda item: self.swap(item, mask), value)

    def tokens_send(self, value, mask, lane, inner=1):
        width = value.shape[-1]
        split = value.reshape(-1, 2, inner * self.own_rows, width)
        bit = self.bit(mask)
        mine = lax.dynamic_index_in_dim(split, bit, 1, keepdims=False).reshape(-1, width)
        sent = lax.dynamic_index_in_dim(split, 1 - bit, 1, keepdims=False).reshape(-1, width)
        return (mine, self.on(lane, sent, mask))

    def tokens_merge(self, mine, got, mask, groups=1):
        part = mine.shape[-1] // groups
        return jnp.concatenate(
            [
                self.ordered(
                    mine[:, i * part : (i + 1) * part], got[:, i * part : (i + 1) * part], mask, 1
                )
                for i in range(groups)
            ],
            axis=1,
        )

    def features_send(self, value, mask, lane, groups=1):
        width = value.shape[2] // (2 * groups)
        bit = self.bit(mask)

        def pick(side):
            return jnp.concatenate(
                [
                    lax.dynamic_slice_in_dim(value, (2 * i + side) * width, width, 2)
                    for i in range(groups)
                ],
                axis=2,
            )

        return (pick(bit), self.on(lane, pick(1 - bit), mask))

    def features_merge(self, mine, got, mask, axis):
        value = self.ordered(jnp.expand_dims(mine, axis), jnp.expand_dims(got, axis), mask, axis)
        return value.reshape(-1, *mine.shape[1:])

    def ordered(self, mine, got, mask, axis):
        low = self.bit(mask) == 0
        return jnp.concatenate(
            [jnp.where(low, mine, got), jnp.where(low, got, mine)], axis=axis
        )

    def all_features(self, value, lane_of):
        for mask in self.rest + [self.b, self.a]:
            value = self.ordered(value, self.on(lane_of(mask), value, mask), mask, 1)
        return value


    def blocks(self, value, pieces, axis):
        size = pieces[0].shape[axis] // self.rows
        found = []
        for step in range(self.rows):
            at = ((self.row - 1 - step + 2 * self.rows) % self.rows) * size
            found.append(
                jnp.concatenate(
                    [lax.dynamic_slice_in_dim(item, at, size, axis) for item in pieces], axis=value
                )
            )
        return found

    def parts(self, sums, mask):
        width = sums.shape[1] // 2
        bit = self.bit(mask)
        return (
            lax.dynamic_slice_in_dim(sums, bit * width, width, 1),
            lax.dynamic_slice_in_dim(sums, (1 - bit) * width, width, 1),
        )

    def halve(self, sums, mask, lane):
        mine, sent = self.parts(sums, mask)
        return mine + self.on(lane, sent, mask)

    def row_sum(self, value):
        mask = 1
        while mask < self.rows:
            pairs = [(i, i ^ mask) for i in range(self.rows)]
            value = value + lax.ppermute(value, "row", pairs)
            mask *= 2
        return value


def norm_forward(residual, gain, shift):
    mean = jnp.mean(residual, axis=1, keepdims=True)
    center = residual - mean
    inverse = lax.rsqrt(jnp.mean(center * center, axis=1, keepdims=True) + EPSILON)
    normed = center * inverse
    return (normed * gain + shift, normed, inverse)


def norm_backward(grad, normed, inverse, gain):
    scaled = grad * gain
    mean = jnp.mean(scaled, axis=1, keepdims=True)
    along = jnp.mean(scaled * normed, axis=1, keepdims=True)
    result = inverse * (scaled - mean - normed * along)
    return (result, jnp.sum(grad * normed, axis=0), jnp.sum(grad, axis=0))


def gelu(value):
    return jax.nn.gelu(value, approximate=True)


def gelu_slope(value):
    inner = 0.7978845608028654
    cubic = 0.044715
    square = value * value
    tangent = jnp.tanh(inner * value * (1.0 + cubic * square))
    return 0.5 * (1.0 + tangent) + 0.5 * value * (1.0 - tangent * tangent) * inner * (
        1.0 + 3.0 * cubic * square
    )


class Clock:
    def __init__(self):
        self.last = None

    def hold(self, value, *others):
        return after(value, self.last, *others)

    def run(self, work, *args):
        self.last = work(*self.hold(args))
        return self.last

    def wait(self, *results):
        self.last = (self.last, results)

    def aside(self, work, *args):
        return work(*self.hold(args))


class Lane:
    def __init__(self, clock, width=1):
        self.clock = clock
        self.width = width
        self.done = []

    def send(self, move, value):
        wait = self.done[-self.width] if len(self.done) >= self.width else None
        result = move(after(value, wait))
        self.done.append(result)
        return result


class Weights:
    def __init__(self, place, clock, ring, blocks):
        self.place, self.clock, self.ring = place, clock, ring
        self.entries = blocks
        self.own = {name: [entry[1]] for name, entry in blocks.items()}
        self.other = {name: [] for name in blocks}
        self.wholes = {}

    def exchange(self, name):
        whole, block, far, lane, axis, corner, spans = self.entries[name]
        step = len(self.other[name])
        self.other[name].append(
            lane.send(lambda value: self.place.swap(value, far), self.own[name][step])
        )

    def exchange_all(self, name):
        whole, block, far, lane, axis, corner, spans = self.entries[name]
        blocks = jnp.concatenate(self.own[name], axis=0)
        got = lane.send(lambda value: self.place.swap(value, far), blocks)
        self.other[name] = jnp.split(got, self.place.rows, axis=0)

    def step(self, name):
        self.own[name].append(self.ring.send(self.place.shift, self.own[name][-1]))

    def arrived(self, step, *names):
        self.clock.wait([self.own[name][step] for name in names])

    def put(self, name, step, side):
        place = self.place
        whole, block, far, lane, axis, corner, spans = self.entries[name]
        items = self.other if side else self.own
        at = ((place.row - step + place.rows) % place.rows) * spans[axis] + corner[axis]
        start = [0, 0]
        start[axis] = at
        start[1 - axis] = side * spans[1 - axis] + corner[1 - axis]
        if whole not in self.wholes:
            shape = [0, 0]
            shape[axis], shape[1 - axis] = place.rows * spans[axis], 2 * spans[1 - axis]
            self.wholes[whole] = jnp.full(shape, len(self.wholes), block.dtype)
        self.wholes[whole] = self.clock.run(
            lambda total, item: lax.dynamic_update_slice(total, item, start),
            self.wholes[whole],
            items[name][step],
        )


def entry(name, block, far, lane, axis):
    return {name: (name, block, far, lane, axis, (0, 0), block.shape)}


def halves(name, block, far, lane, axis):
    half = block.shape[0] // 2
    return {
        name + "0": (name, block[:half], far, lane, axis, (0, 0), block.shape),
        name + "1": (name, block[half:], far, lane, axis, (half, 0), block.shape),
    }


def join(pair):
    return jnp.concatenate(pair, axis=0)


def columns(pair, split):
    return (join([item[:, :split] for item in pair]), join([item[:, split:] for item in pair]))


class Exchange:
    def __init__(self, place, clock, lane, far):
        self.place, self.clock, self.lane, self.bit = place, clock, lane, far

    def far(self, value):
        return self.lane.send(lambda item: self.place.swap(item, self.bit), value)

    def near(self, value):
        for mask in self.place.rest:
            value = self.clock.run(
                lambda own, got: jnp.concatenate([own, got], axis=0),
                value,
                self.place.swap(self.clock.hold(value), mask),
            )
        return value

    def halved(self, terms):
        for mask in self.place.rest[::-1]:
            half = terms.shape[0] // 2
            got = self.place.swap(self.clock.hold(terms[half:]), mask)
            if mask == self.place.rest[0]:
                return (terms[:half], got)
            terms = self.clock.run(
                lambda own, more: (own.astype(f32) + more.astype(f32)).astype(bf16),
                terms[:half],
                got,
            )
        return (terms, jnp.zeros_like(terms))

    def sum_far(self, terms, meanwhile=None):
        kept, got = self.halved(terms)
        if meanwhile is not None:
            meanwhile()
        part = self.clock.run(
            lambda own, more: (own.astype(f32) + more.astype(f32)).astype(bf16), kept, got
        )
        return self.far(part)


def plus(*items):
    total = items[0].astype(f32)
    for item in items[1:]:
        total = total + item.astype(f32)
    return total


def local(
    mesh,
    tokens,
    cotangent,
    segments,
    query_weight,
    query_bias,
    key_weight,
    value_weight,
    value_bias,
    output_weight,
    output_bias,
    first_gain,
    first_shift,
    up_weight,
    up_bias,
    down_weight,
    down_bias,
    second_gain,
    second_shift,
):
    place = Place(mesh, tokens.shape[0] // mesh.shape["col"])
    clock = Clock()
    run = clock.run
    rows = place.rows
    steps = range(1, rows)
    span = query_weight.shape[1]
    hidden_span = up_weight.shape[1]
    own_rows = place.own_rows
    lane_a, lane_b, row_lane = Lane(clock), Lane(clock), Lane(clock)
    across_b = Exchange(place, clock, lane_b, place.b)
    across_a = Exchange(place, clock, lane_a, place.a)

    def on_lane(mask):
        return lane_a if mask == place.a else lane_b if mask == place.b else None

    def project(rows_in, weight, bias):
        return (dot(rows_in, weight) + bias).astype(bf16)

    def up_product(rows_in, weight, bias):
        hidden = dot(rows_in, weight) + bias
        return (hidden, gelu(hidden).astype(bf16))

    def product(rows_in, weight):
        return dot(rows_in, weight).astype(bf16)

    def norm(residual, kept, got, sent, bias, gain, shift):
        result, normed, inverse = norm_forward(plus(residual, kept, got, sent) + bias, gain, shift)
        return (result, result.astype(bf16), normed, inverse)

    w_all = jnp.concatenate([query_weight, key_weight, value_weight], axis=1)
    ring = Weights(
        place,
        clock,
        row_lane,
        {
            **entry("qkv", w_all, place.a, lane_a, 0),
            **entry("out", output_weight, place.a, lane_a, 1),
            **entry("up", up_weight, place.b, lane_b, 0),
            **halves("down", down_weight, place.b, lane_b, 1),
        },
    )

    def steps_of(*names):
        for name in names:
            ring.step(name)

    def exchanges(*names):
        for name in names:
            ring.exchange(name)

    def puts(step, side, *names):
        for name in names:
            ring.put(name, step, side)

    def merge(mask, groups=1):
        return lambda mine, got: place.tokens_merge(mine, got, mask, groups)

    def blocks(*pieces):
        return place.blocks(0, pieces, 1)

    exchanges("qkv")
    steps_of("qkv")
    value = tokens
    for mask in place.rest:
        value = run(merge(mask), *place.tokens_send(value, mask, None))
    value = place.tokens_send(value, place.b, lane_b)
    vectors = jnp.stack(
        [output_bias, first_gain, first_shift, down_bias, second_gain, second_shift]
    )
    for mask in place.rest:
        vectors = place.ordered(vectors, place.swap(vectors, mask), mask, 1)
    got, up_bias_other = lane_b.send(
        lambda items: tuple(place.swap(item, place.b) for item in items), (vectors, up_bias)
    )
    vectors = place.ordered(vectors, got, place.b, 1)
    b_up = jnp.concatenate([up_bias, up_bias_other])
    exchanges("up")
    puts(0, 0, "qkv", "out")
    masks = place.order + [item ^ place.b for item in place.order]
    docs = jnp.concatenate(
        [
            lax.dynamic_slice_in_dim(
                segments, jnp.bitwise_xor(place.col, mask) * own_rows, own_rows, 0
            )
            for mask in masks
        ]
    )
    docs = (docs[None, :], docs[:, None])
    value = run(merge(place.b), *value)
    value = place.tokens_send(value, place.a, lane_a)
    ring.arrived(1, "qkv")
    steps_of("qkv")
    puts(0, 1, "qkv")
    pair = jnp.concatenate([query_bias, jnp.zeros_like(query_bias), value_bias])
    pair_other, got = lane_a.send(
        lambda items: tuple(place.swap(item, place.a) for item in items), (pair, vectors)
    )
    b_qkv = jnp.concatenate([pair, pair_other])
    vectors = place.ordered(vectors, got, place.a, 1)
    b_out, gain1, shift1, b_down, gain2, shift2 = (vectors[i] for i in range(6))
    puts(1, 0, "qkv")
    for step in range(1, rows):
        exchanges("qkv")
        if step < rows - 2:
            steps_of("qkv")
    state_low = run(merge(place.a), *value)
    state = state_low.astype(f32)
    far = across_b.far(state_low)
    exchanges("down0", "down1")
    own = across_b.near(state_low)
    clock.wait(b_qkv, b_up, vectors)
    for step in range(2, rows):
        ring.arrived(step, "qkv")
        if step == rows - 1:
            steps_of("out")
        puts(step, 0, "qkv")
        puts(step - 1, 1, "qkv")
    for step in range(1, rows):
        ring.arrived(step, "out")
        steps_of("out" if step < rows - 1 else "up")
        puts(step, 0, "out")
    ring.exchange_all("out")
    other = across_b.near(far)
    puts(0, 0, "up")
    puts(0, 1, "up")
    puts(rows - 1, 1, "qkv")
    w_qkv = ring.wholes["qkv"]
    clock.wait(ring.other["down0"][0])
    qkv_own = run(project, own, w_qkv, b_qkv)
    ring.arrived(1, "up")
    steps_of("up")
    clock.wait(ring.other["down1"][0])
    exchanges("up")
    qkv_other = run(project, other, w_qkv, b_qkv)
    qkv = run(lambda *items: join(items), qkv_own, qkv_other)
    puts(1, 0, "up")
    ring.arrived(2, "up")
    steps_of("up" if rows > 3 else "down0")
    mixed, log_total = run(lambda item: attend(item, span, *docs), qkv)
    clock.wait(ring.other["up"][1])
    for step in range(rows):
        puts(step, 1, "out")
    w_out = ring.wholes["out"]
    half = mixed.shape[0] // 2
    terms_other = run(product, mixed[half:], w_out)
    terms_own = []

    def meanwhile():
        terms_own.append(run(product, mixed[:half], w_out))
        puts(1, 1, "up")

    sent = across_b.sum_far(terms_other, meanwhile)
    sums = across_b.halved(terms_own[0])
    exchanges("up")
    puts(2, 0, "up")
    for step in range(3, rows):
        ring.arrived(step, "up")
        steps_of("up" if step < rows - 1 else "down0")
        exchanges("up")
        puts(step, 0, "up")
    puts(0, 0, "down0", "down1")
    puts(0, 1, "down0", "down1")
    far_half = ring.entries["down1"]
    corner = (far_half[5][0] + far_half[6][0], 0)
    ring.entries["more"] = (*far_half[:5], corner, far_half[6])
    ring.own["more"] = ring.other["down1"]
    queue = ["down0"] * (rows - 2) + ["down1", "more"] * (rows - 1)
    first, first_low, normed1, inverse1 = run(norm, state, *sums, sent, b_out, gain1, shift1)
    far = across_a.far(first_low)
    ring.arrived(1, "down0")
    steps_of(queue.pop(0))
    exchanges("down0")
    own_first = across_a.near(first_low)
    puts(2, 1, "up")
    puts(1, 0, "down0")
    ring.arrived(2, "down0")
    steps_of(queue.pop(0))
    exchanges("down0")
    puts(2, 0, "down0")
    other_first = across_a.near(far)
    for step in range(3, rows):
        ring.arrived(step, "down0")
        steps_of(queue.pop(0))
        exchanges("down0")
        puts(step, 1, "up")
        puts(step, 0, "down0")
    w_up = ring.wholes["up"]
    ring.arrived(1, "down1")
    steps_of(queue.pop(0))
    hidden_own, active_own = run(up_product, own_first, w_up, b_up)
    ring.arrived(1, "more")
    steps_of(queue.pop(0))
    hidden_other, active_other = run(up_product, other_first, w_up, b_up)
    ring.arrived(2, "down1")
    steps_of(queue.pop(0))
    puts(1, 1, "down0")
    puts(1, 0, "down1", "more")
    token_pieces = run(blocks, own, other)
    ring.arrived(2, "more")
    if queue:
        steps_of(queue.pop(0))
    puts(2, 1, "down0")
    puts(2, 0, "down1", "more")
    first_pieces = run(blocks, own_first, other_first)
    for step in range(3, rows):
        ring.arrived(step, "down1")
        if queue:
            steps_of(queue.pop(0))
        puts(step, 1, "down0")
        puts(step, 0, "down1")
        if step == 3:
            active_sides = run(
                lambda *items: columns(items, hidden_span), active_own, active_other
            )
        ring.arrived(step, "more")
        if queue:
            steps_of(queue.pop(0))
        if step < rows - 1:
            puts(step, 0, "more")
    if rows > 3:
        puts(rows - 1, 0, "more")
    w_down = ring.wholes["down"]
    terms_other = run(product, active_other, w_down)
    sent = across_a.sum_far(terms_other)
    terms_own = run(product, active_own, w_down)
    sums = across_a.halved(terms_own)
    kept_attention = [(token_pieces, qkv, mixed, log_total, normed1, inverse1)]
    state, state_low, normed2, inverse2 = run(
        norm, first, *sums, sent, b_down, gain2, shift2
    )
    kept_feed = [(first_pieces, (hidden_own, hidden_other), active_sides, normed2, inverse2)]

    grad = cotangent
    for mask in place.rest:
        grad = clock.aside(merge(mask), *place.tokens_send(grad, mask, None))
    for depth in range(1, LAYERS):
        far = across_b.far(state_low)
        own = across_b.near(state_low)
        qkv_own = run(project, own, w_qkv, b_qkv)
        other = across_b.near(far)
        qkv_other = run(project, other, w_qkv, b_qkv)
        qkv = run(lambda *items: join(items), qkv_own, qkv_other)
        if depth == 1:
            grad = place.tokens_send(grad, place.a, lane_a, 2)
        mixed, log_total = run(lambda item: attend(item, span, *docs), qkv)
        if depth == 1:
            clock.wait(grad[1])
        terms_other = run(product, mixed[half:], w_out)
        terms_own = []
        sent = across_b.sum_far(
            terms_other, lambda: terms_own.append(run(product, mixed[:half], w_out))
        )
        sums = across_b.halved(terms_own[0])
        token_pieces = run(blocks, own, other)
        if depth == 1:
            grad = run(merge(place.a), *grad)
        first, first_low, normed1, inverse1 = run(norm, state, *sums, sent, b_out, gain1, shift1)
        kept_attention.append((token_pieces, qkv, mixed, log_total, normed1, inverse1))
        far = across_a.far(first_low)
        own = across_a.near(first_low)
        if depth == 1:
            grad = place.tokens_send(grad, place.b, lane_b)
        hidden_own, active_own = run(up_product, own, w_up, b_up)
        terms_own = run(product, active_own, w_down)
        own_sums = across_a.halved(terms_own)
        if depth == 1:
            clock.wait(grad[1])
        other = across_a.near(far)
        hidden_other, active_other = run(up_product, other, w_up, b_up)
        terms_other = run(product, active_other, w_down)
        sent = across_a.sum_far(terms_other)
        if depth == 1:
            grad = run(merge(place.b, 2), *grad)
        first_pieces = run(blocks, own, other)
        active_sides = run(lambda *items: columns(items, hidden_span), active_own, active_other)
        state, state_low, normed2, inverse2 = run(
            norm, first, *own_sums, sent, b_down, gain2, shift2
        )
        kept_feed.append(
            (first_pieces, (hidden_own, hidden_other), active_sides, normed2, inverse2)
        )
    output = state_low[None]

    def gelu_back(rows_in, weight, hidden):
        return (dot_t(rows_in, weight) * gelu_slope(hidden)).astype(bf16)

    def product_t(rows_in, weight):
        return dot_t(rows_in, weight).astype(bf16)

    def norm_back(grads, normed, inverse, gain):
        result, gain_grad, shift_grad = norm_backward(plus(*grads), normed, inverse, gain)
        low = result.astype(bf16)
        return (result, low, jnp.stack([jnp.sum(low, axis=0, dtype=f32), gain_grad, shift_grad]))

    def sum_rows(*items):
        return jnp.concatenate([jnp.sum(item, axis=0, dtype=f32) for item in items])

    class Share:
        def __init__(self, name, left, right, lane, far):
            self.name, self.left, self.right = name, left, right
            self.lane, self.far = lane, far
            self.before = held.get(name)
            self.got = []
            self.sent = []
            self.total = None
            self.step = 0

        def keep(self):
            left, right = clock.hold((self.left, self.right))
            clock.last = [
                [dot_g(left[side][step], right[side][step]) for step in range(rows)]
                for side in (0, 1)
            ]
            held[self.name] = clock.last

        def other_first(self):
            self.other(1)

        def other(self, count=None):
            for step in range(len(self.sent), rows if count is None else count):
                left, right = clock.hold((self.left[1][step], self.right[1][step]))
                clock.last = (dot_g(left, right) + self.before[1][step]).astype(bf16)
                self.sent.append(clock.last)

        def send(self, count=1):
            for step in range(count):
                self.got.append(
                    self.lane.send(
                        lambda item: place.swap(item, self.far), self.sent[len(self.got)]
                    )
                )

        def send_all(self):
            got = self.lane.send(
                lambda item: place.swap(item, self.far), jnp.concatenate(self.sent, axis=0)
            )
            self.got = jnp.split(got, rows, axis=0)

        def advance(self):
            step = self.step
            more = [self.got[step]] + ([] if self.total is None else [self.total])
            left, right, before, more = clock.hold(
                (self.left[0][step], self.right[0][step], self.before[0][step], more)
            )
            value = dot_g(left, right) + before
            for item in more:
                value = value + item.astype(f32)
            self.step += 1
            if step < rows - 1:
                value = value.astype(bf16)
            clock.last = self.result = value
            if step < rows - 1:
                self.total = row_lane.send(place.shift, value)

    held = {}
    norm_sums, qkv_sums, hidden_sums = [], [], []
    grads = (grad,)
    for depth in reversed(range(LAYERS)):
        last = depth == 0
        token_pieces, qkv, mixed, log_total, normed1, inverse1 = kept_attention[depth]
        first_pieces, hiddens, (active_own, active_other), normed2, inverse2 = kept_feed[depth]
        dr2, dsecond, sums2 = run(norm_back, grads, normed2, inverse2, gain2)
        far = across_a.far(dsecond)
        second_own = across_a.near(dsecond)
        if not last:
            output = place.features_send(output, place.b, lane_b, 2)
        dhid_own = run(gelu_back, second_own, w_down, hiddens[0])
        terms_own = run(product_t, dhid_own, w_up)
        own_sums = across_a.halved(terms_own)
        second_other = across_a.near(far)

        def down_share():
            pieces = run(blocks, second_own, second_other)
            return Share(
                "down",
                ([active_own] * rows, [active_other] * rows),
                (pieces, pieces),
                lane_b,
                place.b,
            )

        if last:
            down = down_share()
            down.other()
            down.send(3)
        dhid_other = run(gelu_back, second_other, w_down, hiddens[1])
        terms_other = run(product_t, dhid_other, w_up)
        if not last:
            clock.wait(output[1])
            output = clock.aside(lambda *items: place.features_merge(*items, place.b, 1), *output)
        sides = []
        sent = across_a.sum_far(
            terms_other,
            lambda: sides.extend(
                run(lambda *items: columns(items, hidden_span), dhid_own, dhid_other)
            ),
        )
        dhid_left, dhid_right = sides
        if last:
            down.advance()
        up = Share(
            "up",
            (first_pieces, first_pieces),
            ([dhid_left] * rows, [dhid_right] * rows),
            lane_b,
            place.b,
        )
        if last:
            up.other()
            hidden_total = hidden_sums[0] + clock.aside(sum_rows, dhid_left, dhid_right)
        else:
            down = down_share()
            down.keep()
        dr1, dbranch, sums1 = run(norm_back, (dr2, *own_sums, sent), normed1, inverse1, gain1)
        norm_sums.append(jnp.concatenate([sums1, sums2], axis=0))
        far = across_b.far(dbranch)
        branch_own = across_b.near(dbranch)
        dmixed_own = run(product_t, branch_own, w_out)
        if last:
            token_sums = place.halve(sum(norm_sums), place.a, lane_a)
            down.advance()
            down.send(rows - 3)
            up.send()
        else:
            output = place.features_send(output, place.a, lane_a)
            up.keep()
            clock.wait(output[1])
            hidden_sums.append(clock.aside(sum_rows, dhid_left, dhid_right))
        branch_other = across_b.near(far)
        dmixed_other = run(product_t, branch_other, w_out)
        dmixed = run(lambda *items: join(items), dmixed_own, dmixed_other)
        pieces = run(blocks, branch_own, branch_other)
        out = Share(
            "out",
            ([mixed[:, :span]] * rows, [mixed[:, span:]] * rows),
            (pieces, pieces),
            lane_a,
            place.a,
        )
        if last:
            out.other()
            out.send_all()
            down.advance()
            clock.wait(up.got[0])
            up.send()
        else:
            output = clock.aside(lambda *items: place.features_merge(*items, place.a, 0), *output)
        dqkv = run(lambda *items: attend_back(*items, log_total, span, *docs), qkv, dmixed)
        qkv_sums.append(clock.aside(sum_rows, dqkv))
        if last:
            clock.wait(out.got, up.got[1])
            while down.step < rows:
                down.advance()
            up.advance()
        terms_other = run(product_t, dqkv[half:], w_qkv)
        if last:
            both = Share(
                "qkv",
                (token_pieces, token_pieces),
                ([dqkv[:, : 3 * span]] * rows, [dqkv[:, 3 * span :]] * rows),
                lane_a,
                place.a,
            )
            sent = across_b.sum_far(terms_other, both.other_first)
            both.send()
        else:
            terms_own = []
            sent = across_b.sum_far(
                terms_other, lambda: terms_own.append(run(product_t, dqkv[:half], w_qkv))
            )
            own_sums = across_b.halved(terms_own[0])
        if not last:
            both = Share(
                "qkv",
                (token_pieces, token_pieces),
                ([dqkv[:, : 3 * span]] * rows, [dqkv[:, 3 * span :]] * rows),
                lane_a,
                place.a,
            )
        if last:
            both.other()
            clock.wait(both.got[0], sent)
            both.send()
            up.send()
            up.advance()
        if last:
            terms_own = run(product_t, dqkv[:half], w_qkv)
            own_sums = across_b.halved(terms_own)
        else:
            out.keep()
            both.keep()
        grads = (dr1, *own_sums, sent)
    clock.wait(own_sums)
    out.advance()
    clock.wait(up.got[2])
    up.send(rows - len(up.got))
    out.advance()
    both.send()
    both.advance()
    out.advance()
    grad = run(lambda *items: plus(*items).astype(bf16)[None], *grads)
    grad = place.features_send(grad, place.a, lane_a)
    up.advance()
    while out.step < rows:
        out.advance()
    both.send(rows - 3)
    grad = run(lambda *items: place.features_merge(*items, place.a, 0), *grad)
    grad = place.features_send(grad, place.b, lane_b)
    both.advance()
    grad = run(lambda *items: place.features_merge(*items, place.b, 1), *grad)
    for mask in place.rest[::-1]:
        grad = run(
            lambda *items: place.features_merge(*items, mask, 1),
            *place.features_send(grad, mask, None),
        )
    grad_tokens = grad.reshape(-1, span).astype(f32)
    for mask in place.rest[::-1]:
        output = run(
            lambda *items: place.features_merge(*items, mask, 1),
            *place.features_send(output, mask, None),
        )
    output = output.reshape(-1, span)
    qkv_total = sum(qkv_sums)
    qkv_total = qkv_total[: 3 * span] + lane_a.send(
        lambda item: place.swap(item, place.a), qkv_total[3 * span :]
    )
    mine, away = place.parts(token_sums, place.b)
    more = lane_b.send(
        lambda items: tuple(place.swap(item, place.b) for item in items),
        (away, hidden_total[hidden_span:]),
    )
    token_sums = mine + more[0]
    hidden_total = hidden_total[:hidden_span] + more[1]
    for mask in place.rest[::-1]:
        token_sums = place.halve(token_sums, mask, None)
    while both.step < rows - 1:
        both.advance()
        if up.step < rows:
            up.advance()
    sums = place.row_sum(
        jnp.concatenate([token_sums.reshape(-1), qkv_total, hidden_total])
    )
    while up.step < rows:
        up.advance()
    while both.step < rows:
        both.advance()

    token_sums = sums[: 6 * span].reshape(6, span)
    qkv_sums = sums[6 * span : 9 * span]
    hidden_sums = sums[9 * span :]
    qkv = both.result
    return (
        output,
        grad_tokens,
        qkv[:, :span],
        qkv_sums[:span],
        qkv[:, span : 2 * span],
        qkv[:, 2 * span :],
        qkv_sums[2 * span :],
        out.result,
        token_sums[0],
        token_sums[1],
        token_sums[2],
        up.result,
        hidden_sums,
        down.result,
        token_sums[3],
        token_sums[4],
        token_sums[5],
    )


def solution(mesh):
    both, col, back = P("row", "col"), P("col"), P("col", "row")
    return jax.shard_map(
        functools.partial(local, mesh),
        mesh=mesh,
        in_specs=(
            both, both, P("row"), both, col, both, both, col, back, col, col, col, both, col, back,
            col, col, col,
        ),
        out_specs=(
            both, both, both, col, both, both, col, back, col, col, col, both, col, back, col, col,
            col,
        ),
        check_vma=False,
    )
```
